32 devices in a mesh: blk: 4 (over y, x), group: 8 (over z, core).
Axes of the slice: x: 2, y: 2, z: 4, core: 2. Of those that a mesh axis runs over, the one named last changes fastest.
Arguments:
- star_pos: float32 [3, 32768], P(None, 'blk'), may hold values from -6 to 6
- star_vel: float32 [3, 32768], P(None, 'blk'), may hold values from -6 to 6
- star_acc: float32 [3, 32768], P(None, 'blk'), may hold values from -6 to 6
- star_jerk: float32 [3, 32768], P(None, 'blk'), may hold values from -6 to 6
- star_mass: float32 [32768], P('blk'), may hold values from 0.25 to 4
- star_dt: float32 [32768], P('blk'), may hold values from 0.0625 to 1
- active_list: int32 [4, 8, 128], P('blk', 'group'), may hold values from 0 to 8191
- active_count: int32 [4, 8], P('blk', 'group'), may hold values from 1 to 128, 256 in all within a row
Outputs:
- accel_jerk: float32 [4, 8, 6, 128], P('blk', 'group')
The draws below stay inside these ranges and needn't reach their ends.
Inputs may be any that keep to these rules, and one draw needn't show every extreme that they name: `active_list`: only the first active_count slots of a list are active, the rest are ignored; entries may repeat. `active_count`: for each blk index the counts over group sum to 256, and one of them is exactly 128.
All inputs are finite; a program needn't handle non-finite values.
Results may differ from the reference program's by a relative error of at most 0.00012.
Values sent between devices are 32-bit elements; how exact they have to be, the bound alone decides.
No kernel may reach another device: no remote copies, remote signals or barrier semaphores. Data moves between devices by JAX's collectives and lax.ppermute only.
A program may use at most 64 MiB of HBM per device.

```python
import math
import jax
import jax.numpy as jnp
import numpy as np
from jax import lax

STAR_DEV = 8192
ACT_AVG = 32
ACT_MAX = 128
N_STAR = 32768
N_BLK = 4
N_GROUP = 8


def plant(values, key, low, largest):
    dims = values.shape
    index_at = [jax.random.randint(jax.random.fold_in(key, axis), (), 0, dims[axis]) for axis in range(len(dims))]
    values = values.at[tuple(index_at)].set(low)
    longest = dims.index(max(dims))
    index_at[longest] = (index_at[longest] + 1) % dims[longest]
    return values.at[tuple(index_at)].set(largest)


def block_scale(stream_key, shape, pieces, least, high):
    factor_of, own = 1.0, jax.random.fold_in(stream_key, 6)
    for position, blocks in pieces:
        heights = jnp.exp(jax.random.uniform(jax.random.fold_in(own, position), (blocks,), jnp.float32, least / len(pieces), high / len(pieces)))
        factor_of = factor_of * jnp.repeat(heights, shape[position] // blocks).reshape([-1 if axis == position else 1 for axis in range(len(shape))])
    return factor_of


def rank_bounds(amount, skew):
    weights = [(1 << 20) // math.isqrt(standing ** skew) + 1 for standing in range(1, amount + 1)]
    scale = 1 + sum(weights) // (1 << 30)
    return np.cumsum(np.array([max(1, weight // scale) for weight in weights]))


def skewed_ids(stream_key, dims, amount, skew):
    grid = rank_bounds(amount, skew)
    ticket = jax.random.randint(jax.random.fold_in(stream_key, 1), dims, 0, int(grid[amount - 1]))
    rank = jnp.searchsorted(jnp.asarray(grid, jnp.int32), ticket, side="right")
    return jax.random.permutation(jax.random.fold_in(stream_key, 2), amount)[rank].astype(jnp.int32)


def split_up(number_of, total, most, slope):
    portions = [(1 << 20) // math.isqrt(grade ** slope) + 1 for grade in range(2, number_of + 1)]
    spare, counts = total - most - (number_of - 1), [1] * (number_of - 1)
    while spare > 0:
        candidates = [i for i in range(number_of - 1) if counts[i] < most]
        mass, remaining = sum([portions[i] for i in candidates]), spare
        for i in candidates:
            extra = min(most - counts[i], max(1, remaining * portions[i] // mass), spare)
            counts[i] = counts[i] + extra
            spare = spare - extra
    return np.array([most] + counts)


def uneven(own_key, count, total, limit, skew):
    if count == 2:
        one = jax.random.randint(own_key, (), max(1, total - limit), min(limit, total - 1) + 1)
        return jnp.stack([one, total - one])
    tallies = jnp.asarray(split_up(count, total, limit, skew), jnp.int32)
    couples = (count - 1) // 2
    source_of, receiver = tallies[1:1 + 2 * couples:2], tallies[2:2 + 2 * couples:2]
    room = jnp.minimum(source_of - 1, limit - receiver)
    shifted = jax.random.randint(jax.random.fold_in(own_key, 1), (couples,), 0, 1 << 20) % (room + 1)
    tallies = tallies.at[1:1 + 2 * couples:2].set(source_of - shifted).at[2:2 + 2 * couples:2].set(receiver + shifted)
    return tallies[jax.random.permutation(jax.random.fold_in(own_key, 2), count)]


def scatter_about(rng, extent, spread, reach, split=(), kind=jnp.bfloat16):
    drawn = spread * jax.random.normal(rng, extent, jnp.float32)
    if split:
        drawn = drawn * block_scale(rng, extent, split, -0.22, 0.18)
    return jnp.clip(drawn, -reach, reach).astype(kind)


def setup_inputs(seed: int = 0) -> dict:
    key_list = jax.random.split(jax.random.key(seed), 9)
    star_pos = scatter_about(key_list[0], (3, N_STAR), 1.0, 6.0, ((1, 4),), jnp.float32)
    star_vel = scatter_about(key_list[1], (3, N_STAR), 0.5, 6.0, ((1, 4),), jnp.float32)
    star_acc = scatter_about(key_list[2], (3, N_STAR), 1.0, 6.0, ((1, 4),), jnp.float32)
    star_jerk = scatter_about(key_list[3], (3, N_STAR), 2.0, 6.0, ((1, 4),), jnp.float32)
    star_mass = jnp.clip(jnp.exp(math.log(4.0) - 2.7725887 * jax.random.uniform(key_list[4], (N_STAR,), jnp.float32) ** block_scale(key_list[4], (N_STAR,), ((0, 4),), -0.2, 0.2)), 0.25, 4.0)
    star_dt = jnp.clip(jnp.exp(math.log(1.0) - 2.7725887 * jax.random.uniform(key_list[5], (N_STAR,), jnp.float32) ** block_scale(key_list[5], (N_STAR,), ((0, 4),), -0.2, 0.2)), 0.0625, 1.0)
    active_list = plant(skewed_ids(key_list[6], (N_BLK, N_GROUP, ACT_MAX), STAR_DEV, 2), jax.random.fold_in(key_list[6], 3), 0, STAR_DEV - 1).astype(jnp.int32)
    active_count = jax.vmap(lambda own: uneven(own, N_GROUP, ACT_AVG * N_GROUP, ACT_MAX, 2))(jax.random.split(key_list[7], N_BLK)).reshape((N_BLK, N_GROUP)).astype(jnp.int32)
    return dict(star_pos=star_pos, star_vel=star_vel, star_acc=star_acc, star_jerk=star_jerk, star_mass=star_mass, star_dt=star_dt, active_list=active_list, active_count=active_count)


soften = 0.01

def predict(pos, vel, acc, jerk, delta):
    step = delta[None, :]
    ppos = pos + step * (vel + step * (0.5 * acc + step * (jerk / 6.0)))
    pvel = vel + step * (acc + step * (0.5 * jerk))
    return (ppos, pvel)

def pair_block(rows, stars):
    gap = stars[0:3, None, :] - rows[0:3, :, None]
    drift = stars[3:6, None, :] - rows[3:6, :, None]
    inverse = lax.rsqrt(lax.optimization_barrier(jnp.sum(gap * gap, 0)) + soften)
    cube = stars[6][None, :] * inverse * inverse * inverse
    radial = 3.0 * lax.optimization_barrier(jnp.sum(gap * drift, 0)) * inverse * inverse
    accel = lax.optimization_barrier(jnp.sum(gap * cube[None], 2))
    jerks = lax.optimization_barrier(jnp.sum((drift - radial[None] * gap) * cube[None], 2))
    return jnp.concatenate([accel, jerks], 0)

def pair_sum(rows, stars):
    count = stars.shape[1]
    tile_size = max(128, 262144 // rows.shape[1])
    if count > tile_size and count % tile_size == 0:

        def advance(total, index):
            piece = lax.dynamic_slice_in_dim(stars, index * tile_size, tile_size, 1)
            return (total + pair_block(rows, piece), None)
        total, _ = lax.scan(advance, jnp.zeros((6, rows.shape[1]), jnp.float32), jnp.arange(count // tile_size))
        return total
    return pair_block(rows, stars)

def reference(star_pos, star_vel, star_acc, star_jerk, star_mass, star_dt, active_list, active_count):
    ppos, pvel = predict(star_pos, star_vel, star_acc, star_jerk, star_dt)
    weight = star_mass / N_STAR
    stars = jnp.concatenate([ppos, pvel, weight[None, :]], 0)
    offsets = (jnp.arange(N_BLK, dtype=jnp.int32) * STAR_DEV)[:, None, None]
    global_index = (active_list + offsets).reshape(-1).astype(jnp.int32)
    rows = jnp.take(jnp.concatenate([ppos, pvel], 0), global_index, axis=1)
    blocks = global_index.shape[0] // 1024

    def one_block(index):
        piece = lax.dynamic_slice_in_dim(rows, index * 1024, 1024, 1)
        return pair_sum(piece, stars)
    result = lax.map(one_block, jnp.arange(blocks))
    result = jnp.moveaxis(result, 0, 1).reshape(6, N_BLK, N_GROUP, ACT_MAX)
    result = jnp.transpose(result, (1, 2, 0, 3))
    live = jnp.arange(ACT_MAX, dtype=jnp.int32)[None, None, None, :] < active_count[:, :, None, None]
    return jnp.where(live, result, jnp.zeros_like(result))
```

```python
import functools

import jax
import jax.numpy as jnp
from jax import lax
from jax.experimental import pallas as pl
from jax.experimental.pallas import tpu as pltpu
from jax.sharding import PartitionSpec as P

LANES = 128
SOFTEN = 0.01
VMEM_LIMIT = 48 * 1024 * 1024


def predict_chunk(pos, vel, acc, jerk, mass, delta, chunk, total_stars):
    lanes = pl.ds(pl.multiple_of(chunk * LANES, LANES), LANES)
    step = delta[pl.ds(chunk, 1), :]
    p, v, a, j = pos[:, lanes], vel[:, lanes], acc[:, lanes], jerk[:, lanes]
    ppos = p + step * (v + step * (0.5 * a + step * (j / 6.0)))
    pvel = v + step * (a + step * (0.5 * j))
    weight = mass[pl.ds(chunk, 1), :] / total_stars
    return jnp.concatenate([ppos, pvel, weight, weight], 0)


def send_kernel(total_stars, pos, vel, acc, jerk, mass, delta, half_out):
    chunks = half_out.shape[0] // 8
    base = lax.rem(lax.axis_index("group"), 2) * chunks

    def one(c, _):
        state = predict_chunk(pos, vel, acc, jerk, mass, delta, base + c, total_stars)
        half_out[pl.ds(pl.multiple_of(c * 8, 8), 8), :] = state
        return _

    lax.fori_loop(0, chunks, one, 0, unroll=4)


def pair_terms(rows, stars, base, total):
    star = [stars[pl.ds(base + i, 1), :] for i in range(7)]
    dx, dy, dz, ux, uy, uz = (star[i] - rows[i] for i in range(6))
    inverse = lax.rsqrt(dx * dx + dy * dy + dz * dz + SOFTEN)
    square = inverse * inverse
    cube = (star[6] * inverse) * square
    radial = (3.0 * (dx * ux + dy * uy + dz * uz)) * square
    terms = (
        dx * cube,
        dy * cube,
        dz * cube,
        (ux - radial * dx) * cube,
        (uy - radial * dy) * cube,
        (uz - radial * dz) * cube,
    )
    return tuple(t + x for t, x in zip(total, terms))


def add_forces(splat, star_refs, sums, first, count, fresh):
    def group(g, _):
        place = pl.multiple_of(first + g * 8, 8)
        rows = [splat[pl.ds(place * 8 + i, 8, stride=8), :] for i in range(6)]
        if fresh:
            total = tuple(jnp.zeros((8, LANES), jnp.float32) for _ in range(6))
        else:
            total = tuple(sums[i, pl.ds(place, 8), :] for i in range(6))
        for stars in star_refs:
            total = lax.fori_loop(
                0,
                stars.shape[0] // 8,
                lambda c, t, stars=stars: pair_terms(rows, stars, c * 8, t),
                total,
                unroll=8,
            )
        for i in range(6):
            sums[i, pl.ds(place, 8), :] = total[i]
        return _

    lax.fori_loop(0, (count + 7) // 8, group, 0)


def own_kernel(
    total_stars,
    slots,
    lists,
    counts,
    pos,
    vel,
    acc,
    jerk,
    mass,
    delta,
    half,
    splat,
    sums,
    shard,
):
    def one(c, _):
        state = predict_chunk(pos, vel, acc, jerk, mass, delta, c, total_stars)
        shard[pl.ds(pl.multiple_of(c * 8, 8), 8), :] = state
        return _

    lax.fori_loop(0, shard.shape[0] // 8, one, 0, unroll=4)
    for owner in range(2):

        def fetch(g, _, owner=owner):
            for k in range(8):
                slot = g * 8 + k
                star = lists[owner, slot]
                state = shard[pl.ds(pl.multiple_of(star // LANES * 8, 8), 8), :]
                lane = jnp.full((8, LANES), star % LANES, jnp.int32)
                place = pl.multiple_of((owner * slots + slot) * 8, 8)
                splat[pl.ds(place, 8), :] = jnp.take_along_axis(state, lane, axis=1)
            return _

        lax.fori_loop(0, (counts[owner] + 7) // 8, fetch, 0)
    for owner in range(2):
        add_forces(splat, [half], sums, owner * slots, counts[owner], True)


def far_kernel(slots, n_far, counts, splat, partial, *refs):
    star_refs, (out, sums) = refs[:n_far], refs[n_far:]
    for owner in range(2):
        add_forces(splat, star_refs, sums, owner * slots, counts[owner], True)
    for owner in range(2):
        part = pl.ds(owner * slots, slots)
        for i in range(6):
            whole = sums[i, part, :] + partial[i, part, :]
            out[pl.ds(i, 1), part] = jnp.sum(whole, axis=1)[None, :]


def on_device(
    star_pos, star_vel, star_acc, star_jerk, star_mass, star_dt, active_list, active_count
):
    n_blk = lax.axis_size("blk")
    n_group = lax.axis_size("group")
    shard = star_mass.shape[0]
    total_stars = shard * n_blk
    slots = active_list.shape[2]
    chunks = shard // LANES
    rows = 2 * slots
    vmem = pl.BlockSpec(memory_space=pltpu.VMEM)
    smem = pl.BlockSpec(memory_space=pltpu.SMEM)
    params = pltpu.CompilerParams(vmem_limit_bytes=VMEM_LIMIT)
    raw = (
        star_pos,
        star_vel,
        star_acc,
        star_jerk,
        star_mass.reshape(chunks, LANES),
        star_dt.reshape(chunks, LANES),
    )
    pair = [(i, i ^ 1) for i in range(n_group)]
    other_list = lax.ppermute(active_list, "group", pair)
    other_count = lax.ppermute(active_count, "group", pair)
    half = pl.pallas_call(
        functools.partial(send_kernel, total_stars),
        out_shape=jax.ShapeDtypeStruct((chunks * 4, LANES), jnp.float32),
        in_specs=[vmem] * 6,
        out_specs=vmem,
        compiler_params=params,
        name="predict_half",
    )(*raw)
    far = [
        lax.ppermute(half, "blk", [(i, i ^ s) for i in range(n_blk)]) for s in range(1, n_blk)
    ]
    lists = jnp.concatenate([active_list[0], other_list[0]], 0)
    counts = jnp.concatenate([active_count[0], other_count[0]], 0)
    splat, partial = pl.pallas_call(
        functools.partial(own_kernel, total_stars, slots),
        out_shape=(
            jax.ShapeDtypeStruct((rows * 8, LANES), jnp.float32),
            jax.ShapeDtypeStruct((6, rows, LANES), jnp.float32),
        ),
        in_specs=[smem] * 2 + [vmem] * 7,
        out_specs=(vmem, vmem),
        scratch_shapes=[pltpu.VMEM((chunks * 8, LANES), jnp.float32)],
        compiler_params=params,
        name="own_forces",
    )(lists, counts, *raw, half)
    result = pl.pallas_call(
        functools.partial(far_kernel, slots, len(far)),
        out_shape=jax.ShapeDtypeStruct((6, rows), jnp.float32),
        in_specs=[smem] + [vmem] * (2 + len(far)),
        out_specs=vmem,
        scratch_shapes=[pltpu.VMEM((6, rows, LANES), jnp.float32)],
        compiler_params=params,
        name="far_forces",
    )(counts, splat, partial, *far)
    returned = lax.ppermute(result[:, slots:], "group", pair)
    live = jnp.arange(slots, dtype=jnp.int32) < active_count[0, 0]
    output = jnp.where(live[None, :], result[:, :slots] + returned, 0.0)
    return output[None, None]


def solution(mesh):
    return jax.shard_map(
        on_device,
        mesh=mesh,
        in_specs=(
            P(None, "blk"),
            P(None, "blk"),
            P(None, "blk"),
            P(None, "blk"),
            P("blk"),
            P("blk"),
            P("blk", "group", None),
            P("blk", "group"),
        ),
        out_specs=P("blk", "group", None, None),
        check_vma=False,
    )
```

```python
import functools

import jax
import jax.numpy as jnp
from jax import lax
from jax.experimental import pallas as pl
from jax.experimental.pallas import tpu as pltpu
from jax.sharding import PartitionSpec as P

LANES = 128
SOFTEN = 0.01
VMEM_LIMIT = 48 * 1024 * 1024


def predict_chunk(pos, vel, acc, jerk, mass, delta, chunk, total_stars):
    lanes = pl.ds(pl.multiple_of(chunk * LANES, LANES), LANES)
    step = delta[pl.ds(chunk, 1), :]
    p, v, a, j = pos[:, lanes], vel[:, lanes], acc[:, lanes], jerk[:, lanes]
    ppos = p + step * (v + step * (0.5 * a + step * (j / 6.0)))
    pvel = v + step * (a + step * (0.5 * j))
    weight = mass[pl.ds(chunk, 1), :] / total_stars
    return jnp.concatenate([ppos, pvel, weight, weight], 0)


def predict_kernel(total_stars, *refs):
    raw, count, (full, half, packed) = refs[:7], refs[7], refs[8:11]
    held, sems = refs[11:18], refs[18]
    copies = [
        pltpu.make_async_copy(source, target, sems.at[i])
        for i, (source, target) in enumerate(zip(raw, held))
    ]
    for copy in copies:
        copy.start()
    for copy in copies:
        copy.wait()

    def one(c, _):
        state = predict_chunk(*held[:6], c, total_stars)
        full[pl.ds(pl.multiple_of(c * 8, 8), 8), :] = state
        return _

    lax.fori_loop(0, full.shape[0] // 8, one, 0, unroll=8)
    size = half.shape[0]
    base = pl.multiple_of(lax.rem(lax.axis_index("group"), 2) * size, 8)
    half[...] = full[pl.ds(base, size), :]
    packed[0:1, :] = held[6][...]
    packed[1:2, :] = jnp.full((1, LANES), count[0, 0], jnp.int32)


def pair_terms(rows, stars, base, total):
    star = [stars[pl.ds(base + i, 1), :] for i in range(7)]
    dx, dy, dz, ux, uy, uz = (star[i] - rows[i] for i in range(6))
    inverse = lax.rsqrt(dx * dx + dy * dy + dz * dz + SOFTEN)
    square = inverse * inverse
    cube = (star[6] * inverse) * square
    radial = (3.0 * (dx * ux + dy * uy + dz * uz)) * square
    terms = (
        dx * cube,
        dy * cube,
        dz * cube,
        (ux - radial * dx) * cube,
        (uy - radial * dy) * cube,
        (uz - radial * dz) * cube,
    )
    return tuple(t + x for t, x in zip(total, terms))


def add_forces(splat, star_refs, sums, first, count, fresh):
    def group(g, _):
        place = pl.multiple_of(first + g * 8, 8)
        rows = [splat[pl.ds(place * 8 + i, 8, stride=8), :] for i in range(6)]
        if fresh:
            total = tuple(jnp.zeros((8, LANES), jnp.float32) for _ in range(6))
        else:
            total = tuple(sums[i, pl.ds(place, 8), :] for i in range(6))
        for stars in star_refs:
            total = lax.fori_loop(
                0,
                stars.shape[0] // 8,
                lambda c, t, stars=stars: pair_terms(rows, stars, c * 8, t),
                total,
                unroll=8,
            )
        for i in range(6):
            sums[i, pl.ds(place, 8), :] = total[i]
        return _

    lax.fori_loop(0, (count + 7) // 8, group, 0)


def own_kernel(slots, mine, other, full, half, splat, sums):
    for owner, packed in enumerate((mine, other)):
        count = packed[1, 0]

        def fetch(g, _, owner=owner, packed=packed):
            for k in range(16):
                slot = g * 16 + k
                star = packed[0, slot]
                state = full[pl.ds(pl.multiple_of(star // LANES * 8, 8), 8), :]
                lane = jnp.full((8, LANES), star % LANES, jnp.int32)
                place = pl.multiple_of((owner * slots + slot) * 8, 8)
                splat[pl.ds(place, 8), :] = jnp.take_along_axis(state, lane, axis=1)
            return _

        lax.fori_loop(0, (count + 15) // 16, fetch, 0)
        add_forces(splat, [half], sums, owner * slots, count, True)


def far_kernel(slots, n_far, mine, other, splat, partial, *refs):
    star_refs, (out, sums) = refs[:n_far], refs[n_far:]
    for owner, packed in enumerate((mine, other)):
        add_forces(splat, star_refs, sums, owner * slots, packed[1, 0], True)
    for owner in range(2):
        part = pl.ds(owner * slots, slots)
        for i in range(6):
            whole = sums[i, part, :] + partial[i, part, :]
            out[pl.ds(i, 1), part] = jnp.sum(whole, axis=1)[None, :]


def on_device(
    star_pos, star_vel, star_acc, star_jerk, star_mass, star_dt, active_list, active_count
):
    n_blk = lax.axis_size("blk")
    n_group = lax.axis_size("group")
    shard = star_mass.shape[0]
    total_stars = shard * n_blk
    slots = active_list.shape[2]
    chunks = shard // LANES
    rows = 2 * slots
    vmem = pl.BlockSpec(memory_space=pltpu.VMEM)
    smem = pl.BlockSpec(memory_space=pltpu.SMEM)
    params = pltpu.CompilerParams(vmem_limit_bytes=VMEM_LIMIT)
    raw = (
        star_pos,
        star_vel,
        star_acc,
        star_jerk,
        star_mass.reshape(chunks, LANES),
        star_dt.reshape(chunks, LANES),
        active_list[0],
    )
    pair = [(i, i ^ 1) for i in range(n_group)]
    full, half, packed = pl.pallas_call(
        functools.partial(predict_kernel, total_stars),
        out_shape=(
            jax.ShapeDtypeStruct((chunks * 8, LANES), jnp.float32),
            jax.ShapeDtypeStruct((chunks * 4, LANES), jnp.float32),
            jax.ShapeDtypeStruct((2, slots), jnp.int32),
        ),
        in_specs=[pl.BlockSpec(memory_space=pltpu.HBM)] * 7 + [smem],
        out_specs=(vmem, vmem, vmem),
        scratch_shapes=[pltpu.VMEM(x.shape, x.dtype) for x in raw]
        + [pltpu.SemaphoreType.DMA((7,))],
        compiler_params=params,
        name="predict",
    )(*(pltpu.with_memory_space_constraint(x, pltpu.HBM) for x in raw), active_count)
    other = lax.ppermute(packed, "group", pair)
    far = [
        lax.ppermute(half, "blk", [(i, i ^ s) for i in range(n_blk)]) for s in range(1, n_blk)
    ]
    splat, partial = pl.pallas_call(
        functools.partial(own_kernel, slots),
        out_shape=(
            jax.ShapeDtypeStruct((rows * 8, LANES), jnp.float32),
            jax.ShapeDtypeStruct((6, rows, LANES), jnp.float32),
        ),
        in_specs=[smem] * 2 + [vmem] * 2,
        out_specs=(vmem, vmem),
        compiler_params=params,
        name="own_forces",
    )(packed, other, full, half)
    result = pl.pallas_call(
        functools.partial(far_kernel, slots, len(far)),
        out_shape=jax.ShapeDtypeStruct((6, rows), jnp.float32),
        in_specs=[smem] * 2 + [vmem] * (2 + len(far)),
        out_specs=vmem,
        scratch_shapes=[pltpu.VMEM((6, rows, LANES), jnp.float32)],
        compiler_params=params,
        name="far_forces",
    )(packed, other, splat, partial, *far)
    returned = lax.ppermute(result[:, slots:], "group", pair)
    live = lax.broadcasted_iota(jnp.int32, (1, slots), 1) < packed[1:2]
    output = jnp.where(live, result[:, :slots] + returned, 0.0)
    return output[None, None]


def solution(mesh):
    return jax.shard_map(
        on_device,
        mesh=mesh,
        in_specs=(
            P(None, "blk"),
            P(None, "blk"),
            P(None, "blk"),
            P(None, "blk"),
            P("blk"),
            P("blk"),
            P("blk", "group", None),
            P("blk", "group"),
        ),
        out_specs=P("blk", "group", None, None),
        check_vma=False,
    )
```

```python
import functools

import jax
import jax.numpy as jnp
from jax import lax
from jax.experimental import pallas as pl
from jax.experimental.pallas import tpu as pltpu
from jax.sharding import PartitionSpec as P

LANES = 128
LANE_BITS = 7
SOFTEN = 0.01
VMEM_LIMIT = 48 * 1024 * 1024


def predict_chunk(pos, vel, acc, jerk, mass, delta, chunk, total_stars):
    lanes = pl.ds(pl.multiple_of(chunk * LANES, LANES), LANES)
    step = delta[pl.ds(chunk, 1), :]
    p, v, a, j = pos[:, lanes], vel[:, lanes], acc[:, lanes], jerk[:, lanes]
    ppos = p + step * (v + step * (0.5 * a + step * (j / 6.0)))
    pvel = v + step * (a + step * (0.5 * j))
    weight = mass[pl.ds(chunk, 1), :] / total_stars
    return jnp.concatenate([ppos, pvel, weight, weight], 0)


def predict_kernel(total_stars, *refs):
    raw, count, (full, half, packed) = refs[:7], refs[7], refs[8:11]
    held, sems = refs[11:18], refs[18]
    copies = [
        pltpu.make_async_copy(source, target, sems.at[i])
        for i, (source, target) in enumerate(zip(raw, held))
    ]
    for copy in copies:
        copy.start()
    for copy in copies:
        copy.wait()

    def one(c, _):
        state = predict_chunk(*held[:6], c, total_stars)
        full[pl.ds(pl.multiple_of(c * 8, 8), 8), :] = state
        return _

    lax.fori_loop(0, full.shape[0] // 8, one, 0, unroll=8)
    size = half.shape[0]
    base = pl.multiple_of(lax.rem(lax.axis_index("group"), 2) * size, 8)
    half[...] = full[pl.ds(base, size), :]
    packed[0:1, :] = held[6][...]
    packed[1:2, :] = jnp.full((1, LANES), count[0, 0], jnp.int32)


def pair_terms(rows, stars, base, total):
    star = [stars[pl.ds(base + i, 1), :] for i in range(7)]
    dx, dy, dz, ux, uy, uz = (star[i] - rows[i] for i in range(6))
    inverse = lax.rsqrt(dx * dx + dy * dy + dz * dz + SOFTEN)
    square = inverse * inverse
    cube = (star[6] * inverse) * square
    radial = (3.0 * (dx * ux + dy * uy + dz * uz)) * square
    terms = (
        dx * cube,
        dy * cube,
        dz * cube,
        (ux - radial * dx) * cube,
        (uy - radial * dy) * cube,
        (uz - radial * dz) * cube,
    )
    return tuple(t + x for t, x in zip(total, terms))


def add_forces(splat, star_refs, sums, slots, counts):
    groups = [(count + 7) // 8 for count in counts]

    def group(g, _):
        place = g * 8
        passed = groups[0]
        for owner in range(1, len(groups)):
            place = jnp.where(g >= passed, (g - passed) * 8 + owner * slots, place)
            passed = passed + groups[owner]
        place = pl.multiple_of(place, 8)
        rows = [splat[pl.ds(place * 8 + i, 8, stride=8), :] for i in range(6)]
        total = tuple(jnp.zeros((8, LANES), jnp.float32) for _ in range(6))
        for stars in star_refs:
            total = lax.fori_loop(
                0,
                stars.shape[0] // 8,
                lambda c, t, stars=stars: pair_terms(rows, stars, c * 8, t),
                total,
                unroll=32,
            )
        for i in range(6):
            sums[i, pl.ds(place, 8), :] = total[i]
        return _

    lax.fori_loop(0, sum(groups), group, 0)


def own_kernel(slots, mine, other, full, half, splat, sums):
    for owner, packed in enumerate((mine, other)):

        def fetch(g, _, owner=owner, packed=packed):
            for k in range(32):
                slot = g * 32 + k
                star = packed[0, slot]
                chunk = lax.shift_right_logical(star, LANE_BITS)
                state = full[pl.ds(pl.multiple_of(chunk * 8, 8), 8), :]
                lane = jnp.full((8, LANES), star & (LANES - 1), jnp.int32)
                place = pl.multiple_of((owner * slots + slot) * 8, 8)
                splat[pl.ds(place, 8), :] = jnp.take_along_axis(state, lane, axis=1)
            return _

        lax.fori_loop(0, (packed[1, 0] + 31) // 32, fetch, 0)
    add_forces(splat, [half], sums, slots, (mine[1, 0], other[1, 0]))


def far_kernel(slots, n_far, mine, other, splat, partial, *refs):
    star_refs, (out, sums) = refs[:n_far], refs[n_far:]
    add_forces(splat, star_refs, sums, slots, (mine[1, 0], other[1, 0]))
    for owner in range(2):
        part = pl.ds(owner * slots, slots)
        for i in range(6):
            whole = sums[i, part, :] + partial[i, part, :]
            out[pl.ds(i, 1), part] = jnp.sum(whole, axis=1)[None, :]


def on_device(
    star_pos, star_vel, star_acc, star_jerk, star_mass, star_dt, active_list, active_count
):
    n_blk = lax.axis_size("blk")
    n_group = lax.axis_size("group")
    shard = star_mass.shape[0]
    total_stars = shard * n_blk
    slots = active_list.shape[2]
    chunks = shard // LANES
    rows = 2 * slots
    vmem = pl.BlockSpec(memory_space=pltpu.VMEM)
    smem = pl.BlockSpec(memory_space=pltpu.SMEM)
    params = pltpu.CompilerParams(vmem_limit_bytes=VMEM_LIMIT)
    raw = (
        star_pos,
        star_vel,
        star_acc,
        star_jerk,
        star_mass.reshape(chunks, LANES),
        star_dt.reshape(chunks, LANES),
        active_list[0],
    )
    pair = [(i, i ^ 1) for i in range(n_group)]
    full, half, packed = pl.pallas_call(
        functools.partial(predict_kernel, total_stars),
        out_shape=(
            jax.ShapeDtypeStruct((chunks * 8, LANES), jnp.float32),
            jax.ShapeDtypeStruct((chunks * 4, LANES), jnp.float32),
            jax.ShapeDtypeStruct((2, slots), jnp.int32),
        ),
        in_specs=[pl.BlockSpec(memory_space=pltpu.HBM)] * 7 + [smem],
        out_specs=(vmem, vmem, vmem),
        scratch_shapes=[pltpu.VMEM(x.shape, x.dtype) for x in raw]
        + [pltpu.SemaphoreType.DMA((7,))],
        compiler_params=params,
        name="predict",
    )(*(pltpu.with_memory_space_constraint(x, pltpu.HBM) for x in raw), active_count)
    other = lax.ppermute(packed, "group", pair)
    far = [
        lax.ppermute(half, "blk", [(i, i ^ s) for i in range(n_blk)]) for s in range(1, n_blk)
    ]
    splat, partial = pl.pallas_call(
        functools.partial(own_kernel, slots),
        out_shape=(
            jax.ShapeDtypeStruct((rows * 8, LANES), jnp.float32),
            jax.ShapeDtypeStruct((6, rows, LANES), jnp.float32),
        ),
        in_specs=[smem] * 2 + [vmem] * 2,
        out_specs=(vmem, vmem),
        compiler_params=params,
        name="own_forces",
    )(packed, other, full, half)
    result = pl.pallas_call(
        functools.partial(far_kernel, slots, len(far)),
        out_shape=jax.ShapeDtypeStruct((6, rows), jnp.float32),
        in_specs=[smem] * 2 + [vmem] * (2 + len(far)),
        out_specs=vmem,
        scratch_shapes=[pltpu.VMEM((6, rows, LANES), jnp.float32)],
        compiler_params=params,
        name="far_forces",
    )(packed, other, splat, partial, *far)
    returned = lax.ppermute(result[:, slots:], "group", pair)
    live = lax.broadcasted_iota(jnp.int32, (1, slots), 1) < packed[1:2]
    output = jnp.where(live, result[:, :slots] + returned, 0.0)
    return output[None, None]


def solution(mesh):
    return jax.shard_map(
        on_device,
        mesh=mesh,
        in_specs=(
            P(None, "blk"),
            P(None, "blk"),
            P(None, "blk"),
            P(None, "blk"),
            P("blk"),
            P("blk"),
            P("blk", "group", None),
            P("blk", "group"),
        ),
        out_specs=P("blk", "group", None, None),
        check_vma=False,
    )
```

```python
import functools

import jax
import jax.numpy as jnp
from jax import lax
from jax.experimental import pallas as pl
from jax.experimental.pallas import tpu as pltpu
from jax.sharding import PartitionSpec as P

LANES = 128
LANE_BITS = 7
SOFTEN = 0.01
VMEM_LIMIT = 48 * 1024 * 1024
FETCH = 32
SHARERS = 4


def predict_chunk(pos, vel, acc, jerk, mass, delta, chunk, total_stars):
    lanes = pl.ds(pl.multiple_of(chunk * LANES, LANES), LANES)
    step = delta[pl.ds(chunk, 1), :]
    p, v, a, j = pos[:, lanes], vel[:, lanes], acc[:, lanes], jerk[:, lanes]
    ppos = p + step * (v + step * (0.5 * a + step * (j / 6.0)))
    pvel = v + step * (a + step * (0.5 * j))
    weight = mass[pl.ds(chunk, 1), :] / total_stars
    return jnp.concatenate([ppos, pvel, weight, weight], 0)


def predict_kernel(total_stars, *refs):
    raw, count, (full, part, packed) = refs[:7], refs[7], refs[8:11]
    held, sems = refs[11:18], refs[18]
    copies = [
        pltpu.make_async_copy(source, target, sems.at[i])
        for i, (source, target) in enumerate(zip(raw, held))
    ]
    for copy in copies:
        copy.start()
    for copy in copies:
        copy.wait()

    def one(c, _):
        state = predict_chunk(*held[:6], c, total_stars)
        full[pl.ds(pl.multiple_of(c * 8, 8), 8), :] = state
        return _

    lax.fori_loop(0, full.shape[0] // 8, one, 0, unroll=8)
    size = part.shape[0]
    base = pl.multiple_of(lax.rem(lax.axis_index("group"), SHARERS) * size, 8)
    part[...] = full[pl.ds(base, size), :]
    packed[0:1, :] = held[6][...]
    packed[1:2, :] = jnp.full((1, LANES), count[0, 0], jnp.int32)


def pair_terms(rows, stars, base, total):
    star = [stars[pl.ds(base + i, 1), :] for i in range(7)]
    dx, dy, dz, ux, uy, uz = (star[i] - rows[i] for i in range(6))
    inverse = lax.rsqrt(dx * dx + dy * dy + dz * dz + SOFTEN)
    square = inverse * inverse
    cube = (star[6] * inverse) * square
    radial = (3.0 * (dx * ux + dy * uy + dz * uz)) * square
    terms = (
        dx * cube,
        dy * cube,
        dz * cube,
        (ux - radial * dx) * cube,
        (uy - radial * dy) * cube,
        (uz - radial * dz) * cube,
    )
    return tuple(t + x for t, x in zip(total, terms))


def gather(lists, full, splat):
    base = 0
    for owner in range(SHARERS):

        def fetch(g, _, owner=owner, base=base):
            for k in range(FETCH):
                slot = g * FETCH + k
                star = lists[2 * owner, slot]
                chunk = lax.shift_right_logical(star, LANE_BITS)
                state = full[pl.ds(pl.multiple_of(chunk * 8, 8), 8), :]
                lane = jnp.full((8, LANES), star & (LANES - 1), jnp.int32)
                place = pl.multiple_of((base + slot) * 8, 8)
                splat[pl.ds(place, 8), :] = jnp.take_along_axis(state, lane, axis=1)
            return _

        count = lists[2 * owner + 1, 0]
        lax.fori_loop(0, (count + FETCH - 1) // FETCH, fetch, 0)
        base = base + count


def total_count(lists):
    return sum(lists[2 * owner + 1, 0] for owner in range(SHARERS))


def add_forces(count, splat, stars, unroll, before, after):
    def group(g, _):
        place = pl.multiple_of(g * 8, 8)
        rows = [splat[pl.ds(place * 8 + i, 8, stride=8), :] for i in range(6)]
        if before is None:
            total = tuple(jnp.zeros((8, LANES), jnp.float32) for _ in range(6))
        else:
            total = tuple(before[i, pl.ds(place, 8), :] for i in range(6))
        total = lax.fori_loop(
            0,
            stars.shape[0] // 8,
            lambda c, t: pair_terms(rows, stars, pl.multiple_of(c * 8, 8), t),
            total,
            unroll=unroll,
        )
        for i in range(6):
            after[i, pl.ds(place, 8), :] = total[i]
        return _

    lax.fori_loop(0, (count + 7) // 8, group, 0)


def near_kernel(lists, full, part, splat, sums):
    gather(lists, full, splat)
    add_forces(total_count(lists), splat, part, part.shape[0] // 8, None, sums)


def far_kernel(*refs):
    lists, splat, sums = refs[:3]
    parts, outs, (stars, held, flat) = refs[3:-7], refs[-7:-3], refs[-3:]
    slots = outs[0].shape[1]
    size = parts[0].shape[0]
    for i, part in enumerate(parts):
        stars[pl.ds(i * size, size), :] = part[...]
    count = total_count(lists)
    add_forces(count, splat, stars, size * 3 // 16, sums, held)
    for block in range(SHARERS):

        @pl.when(count > block * slots)
        def _():
            part = pl.ds(block * slots, slots)
            for j in range(6):
                flat[pl.ds(j, 1), part] = jnp.sum(held[j, part, :], axis=1)[None, :]

    whole = flat[...]
    width = whole.shape[1]
    first = 0
    for owner, out in enumerate(outs):
        out[...] = (pltpu.roll(whole, width - first, 1) if owner else whole)[:, :slots]
        first = first + lists[2 * owner + 1, 0]


def on_device(
    star_pos, star_vel, star_acc, star_jerk, star_mass, star_dt, active_list, active_count
):
    n_blk = lax.axis_size("blk")
    shard = star_mass.shape[0]
    total_stars = shard * n_blk
    slots = active_list.shape[2]
    chunks = shard // LANES
    room = SHARERS * slots + FETCH
    vmem = pl.BlockSpec(memory_space=pltpu.VMEM)
    smem = pl.BlockSpec(memory_space=pltpu.SMEM)
    params = pltpu.CompilerParams(vmem_limit_bytes=VMEM_LIMIT)
    splat_type = jax.ShapeDtypeStruct((room * 8, LANES), jnp.float32)
    sums_type = jax.ShapeDtypeStruct((6, room, LANES), jnp.float32)
    raw = (
        star_pos,
        star_vel,
        star_acc,
        star_jerk,
        star_mass.reshape(chunks, LANES),
        star_dt.reshape(chunks, LANES),
        active_list[0],
    )

    def swap(x, axis, bits):
        return lax.ppermute(x, axis, [(i, i ^ bits) for i in range(lax.axis_size(axis))])

    part_type = jax.ShapeDtypeStruct((chunks * 8 // SHARERS, LANES), jnp.float32)
    full, part, packed = pl.pallas_call(
        functools.partial(predict_kernel, total_stars),
        out_shape=(
            jax.ShapeDtypeStruct((chunks * 8, LANES), jnp.float32),
            part_type,
            jax.ShapeDtypeStruct((2, slots), jnp.int32),
        ),
        in_specs=[pl.BlockSpec(memory_space=pltpu.HBM)] * 7 + [smem],
        out_specs=(vmem,) * 3,
        scratch_shapes=[pltpu.VMEM(x.shape, x.dtype) for x in raw]
        + [pltpu.SemaphoreType.DMA((7,))],
        compiler_params=params,
        name="predict",
    )(*(pltpu.with_memory_space_constraint(x, pltpu.HBM) for x in raw), active_count)
    parts = [swap(part, "blk", s) for s in range(1, n_blk)]
    lists = [packed] + [swap(packed, "group", bits) for bits in range(1, SHARERS)]
    lists = jnp.concatenate(lists, 0)
    splat, sums = pl.pallas_call(
        near_kernel,
        out_shape=(splat_type, sums_type),
        in_specs=[smem] + [vmem] * 2,
        out_specs=(vmem,) * 2,
        compiler_params=params,
        name="near_forces",
    )(lists, full, part)
    outs = pl.pallas_call(
        far_kernel,
        out_shape=(jax.ShapeDtypeStruct((8, slots), jnp.float32),) * SHARERS,
        in_specs=[smem] + [vmem] * (2 + len(parts)),
        out_specs=(vmem,) * SHARERS,
        scratch_shapes=[
            pltpu.VMEM((len(parts) * part_type.shape[0], LANES), jnp.float32),
            pltpu.VMEM(sums_type.shape, jnp.float32),
            pltpu.VMEM((8, SHARERS * slots), jnp.float32),
        ],
        compiler_params=params,
        name="far_forces",
    )(lists, splat, sums, *parts)
    returned = [swap(x, "group", bits) for bits, x in enumerate(outs) if bits]
    live = lax.broadcasted_iota(jnp.int32, (1, slots), 1) < packed[1:2]
    total = outs[0] + returned[0] + (returned[1] + returned[2])
    output = jnp.where(live, total[:6], 0.0)
    return output[None, None]


def solution(mesh):
    return jax.shard_map(
        on_device,
        mesh=mesh,
        in_specs=(
            P(None, "blk"),
            P(None, "blk"),
            P(None, "blk"),
            P(None, "blk"),
            P("blk"),
            P("blk"),
            P("blk", "group", None),
            P("blk", "group"),
        ),
        out_specs=P("blk", "group", None, None),
        check_vma=False,
    )
```

```python
import functools

import jax
import jax.numpy as jnp
from jax import lax
from jax.experimental import pallas as pl
from jax.experimental.pallas import tpu as pltpu
from jax.sharding import PartitionSpec as P

LANES = 128
LANE_BITS = 7
SOFTEN = 0.01
VMEM_LIMIT = 48 * 1024 * 1024
FETCH = 32
SHARERS = 4


def predict_chunk(pos, vel, acc, jerk, mass, delta, chunk, total_stars):
    lanes = pl.ds(pl.multiple_of(chunk * LANES, LANES), LANES)
    step = delta[pl.ds(chunk, 1), :]
    p, v, a, j = pos[:, lanes], vel[:, lanes], acc[:, lanes], jerk[:, lanes]
    ppos = p + step * (v + step * (0.5 * a + step * (j / 6.0)))
    pvel = v + step * (a + step * (0.5 * j))
    weight = mass[pl.ds(chunk, 1), :] / total_stars
    return jnp.concatenate([ppos, pvel, weight, weight], 0)


def predict_kernel(total_stars, *refs):
    raw, count, (full, part, half, packed) = refs[:7], refs[7], refs[8:12]
    held, sems = refs[12:19], refs[19]
    copies = [
        pltpu.make_async_copy(source, target, sems.at[i])
        for i, (source, target) in enumerate(zip(raw, held))
    ]
    for copy in copies:
        copy.start()
    for copy in copies:
        copy.wait()

    def one(c, _):
        state = predict_chunk(*held[:6], c, total_stars)
        full[pl.ds(pl.multiple_of(c * 8, 8), 8), :] = state
        return _

    lax.fori_loop(0, full.shape[0] // 8, one, 0, unroll=8)
    for out in (part, half):
        size = out.shape[0]
        pieces = full.shape[0] // size
        base = pl.multiple_of(lax.rem(lax.axis_index("group"), pieces) * size, 8)
        out[...] = full[pl.ds(base, size), :]
    packed[...] = jnp.zeros_like(packed)
    packed[0:1, :] = held[6][...]
    packed[1:2, :] = jnp.full((1, LANES), count[0, 0], jnp.int32)


def pair_terms(rows, stars, base, total):
    star = [stars[pl.ds(base + i, 1), :] for i in range(7)]
    dx, dy, dz, ux, uy, uz = (star[i] - rows[i] for i in range(6))
    inverse = lax.rsqrt(dx * dx + dy * dy + dz * dz + SOFTEN)
    square = inverse * inverse
    cube = (star[6] * inverse) * square
    radial = (dx * ux + dy * uy + dz * uz) * square
    ax, ay, az = dx * cube, dy * cube, dz * cube
    terms = (ax, ay, az, ux * cube, uy * cube, uz * cube, radial * ax, radial * ay, radial * az)
    return tuple(t + x for t, x in zip(total, terms))


def gather(lists, full, splat):
    base = 0
    for owner in range(SHARERS):

        def fetch(g, _, owner=owner, base=base):
            for k in range(FETCH):
                slot = g * FETCH + k
                star = lists[2 * owner, slot]
                chunk = lax.shift_right_logical(star, LANE_BITS)
                state = full[pl.ds(pl.multiple_of(chunk * 8, 8), 8), :]
                lane = jnp.full((8, LANES), star & (LANES - 1), jnp.int32)
                place = pl.multiple_of((base + slot) * 8, 8)
                splat[pl.ds(place, 8), :] = jnp.take_along_axis(
                    state, lane, axis=1, mode="promise_in_bounds"
                )
            return _

        count = lists[2 * owner + 1, 0]
        lax.fori_loop(0, (count + FETCH - 1) // FETCH, fetch, 0)
        base = base + count


def group_bounds(lists):
    counts = [lists[2 * owner + 1, 0] for owner in range(SHARERS)]
    there, here = counts[0] + counts[1], counts[2] + counts[3]
    return (jnp.maximum(there, here) + 7) // 8, (there + here + 7) // 8


def add_lanes(begin, end, sums, flat):
    slots = flat.shape[1] // SHARERS
    for block in range(SHARERS):

        @pl.when((end * 8 > block * slots) & (begin * 8 < (block + 1) * slots))
        def _():
            part = pl.ds(block * slots, slots)
            for j in range(6):
                flat[pl.ds(j, 1), part] = jnp.sum(sums[j, part, :], axis=1)[None, :]


def cut(lists, owner, flat, slots):
    first = sum(lists[2 * before + 1, 0] for before in range(owner))
    return pltpu.roll(flat, flat.shape[1] - first, 1)[:, :slots] if owner else flat[:, :slots]


def add_forces(begin, end, splat, stars, unroll, before, after):
    def group(g, _):
        place = pl.multiple_of(g * 8, 8)
        rows = [splat[pl.ds(place * 8 + i, 8, stride=8), :] for i in range(6)]
        if before is None:
            total = tuple(jnp.zeros((8, LANES), jnp.float32) for _ in range(9))
        else:
            total = tuple(before[i, pl.ds(place, 8), :] for i in range(6)) + (
                jnp.zeros((8, LANES), jnp.float32),
            ) * 3
        total = lax.fori_loop(
            0,
            stars.shape[0] // 8,
            lambda c, t: pair_terms(rows, stars, pl.multiple_of(c * 8, 8), t),
            total,
            unroll=unroll,
        )
        for i in range(3):
            after[i, pl.ds(place, 8), :] = total[i]
            after[3 + i, pl.ds(place, 8), :] = total[3 + i] - 3.0 * total[6 + i]
        return _

    lax.fori_loop(begin, end, group, 0)


def near_kernel(lists, full, part, splat, sums):
    gather(lists, full, splat)
    _, groups = group_bounds(lists)
    add_forces(0, groups, splat, part, part.shape[0] // 8, None, sums)


def there_kernel(*refs):
    lists, splat, sums = refs[:3]
    parts, (blocks, flat, stars, held) = refs[3:-4], refs[-4:]
    begin = 0
    for part in parts:
        stars[pl.ds(begin, part.shape[0]), :] = part[...]
        begin += part.shape[0]
    shared, _ = group_bounds(lists)
    add_forces(0, shared, splat, stars, 48, sums, held)
    add_lanes(0, shared, held, flat)
    for owner in range(2):
        blocks[owner * 8 : owner * 8 + 8, :] = cut(lists, owner, flat[...], blocks.shape[1])


def here_kernel(lists, splat, sums, stars, flat, mine, other, held, rest):
    shared, groups = group_bounds(lists)
    add_forces(shared, groups, splat, stars, 48, sums, held)
    add_lanes(shared, groups, held, rest)
    done = lax.broadcasted_iota(jnp.int32, flat.shape, 1) < shared * 8
    whole = jnp.where(done, flat[...], rest[...])
    for owner, out in ((2, mine), (3, other)):
        out[...] = cut(lists, owner, whole, out.shape[1])


def on_device(
    star_pos, star_vel, star_acc, star_jerk, star_mass, star_dt, active_list, active_count
):
    n_blk = lax.axis_size("blk")
    n_group = lax.axis_size("group")
    shard = star_mass.shape[0]
    total_stars = shard * n_blk
    slots = active_list.shape[2]
    chunks = shard // LANES
    room = SHARERS * slots + FETCH
    vmem = pl.BlockSpec(memory_space=pltpu.VMEM)
    smem = pl.BlockSpec(memory_space=pltpu.SMEM)
    params = pltpu.CompilerParams(vmem_limit_bytes=VMEM_LIMIT)
    splat_type = jax.ShapeDtypeStruct((room * 8, LANES), jnp.float32)
    sums_type = jax.ShapeDtypeStruct((6, room, LANES), jnp.float32)
    raw = (
        star_pos,
        star_vel,
        star_acc,
        star_jerk,
        star_mass.reshape(chunks, LANES),
        star_dt.reshape(chunks, LANES),
        active_list[0],
    )

    def swap(x, axis, bits):
        return lax.ppermute(x, axis, [(i, i ^ bits) for i in range(lax.axis_size(axis))])

    def trade(x, step):
        pairs = [
            (b * n_group + g, (b ^ step ^ (2 if g & 2 else 1)) * n_group + g)
            for b in range(n_blk)
            for g in range(n_group)
        ]
        return lax.ppermute(x, ("blk", "group"), pairs)

    part_type = jax.ShapeDtypeStruct((chunks * 8 // SHARERS, LANES), jnp.float32)
    full, part, half, packed = pl.pallas_call(
        functools.partial(predict_kernel, total_stars),
        out_shape=(
            jax.ShapeDtypeStruct((chunks * 8, LANES), jnp.float32),
            part_type,
            jax.ShapeDtypeStruct((chunks * 4, LANES), jnp.float32),
            jax.ShapeDtypeStruct((64, slots), jnp.int32),
        ),
        in_specs=[pl.BlockSpec(memory_space=pltpu.HBM)] * 7 + [smem],
        out_specs=(vmem,) * 4,
        scratch_shapes=[pltpu.VMEM(x.shape, x.dtype) for x in raw]
        + [pltpu.SemaphoreType.DMA((7,))],
        compiler_params=params,
        name="predict",
    )(*(pltpu.with_memory_space_constraint(x, pltpu.HBM) for x in raw), active_count)
    parts = []
    for step in range(0, n_blk, 4):
        parts.append(trade(half, step))
        parts += [swap(part, "blk", bits) for bits in (step + 3, step) if bits]
    core, *others = (swap(packed, "group", bits) for bits in range(1, SHARERS))
    lists = jnp.concatenate([x[:2] for x in (*others, packed, core)], 0)
    splat, sums = pl.pallas_call(
        near_kernel,
        out_shape=(splat_type, sums_type),
        in_specs=[smem] + [vmem] * 2,
        out_specs=(vmem,) * 2,
        compiler_params=params,
        name="near_forces",
    )(lists, full, part)
    block_type = jax.ShapeDtypeStruct((8, slots), jnp.float32)
    pairs = slots * shard
    cost = pl.CostEstimate(flops=40 * pairs, bytes_accessed=pairs, transcendentals=pairs)
    flat_type = jax.ShapeDtypeStruct((8, SHARERS * slots), jnp.float32)
    stars_type = jax.ShapeDtypeStruct((sum(x.shape[0] for x in parts), LANES), jnp.float32)
    there, flat, stars = pl.pallas_call(
        there_kernel,
        out_shape=(
            jax.ShapeDtypeStruct((16, slots), jnp.float32),
            flat_type,
            stars_type,
        ),
        in_specs=[vmem] + [vmem] * (2 + len(parts)),
        out_specs=(vmem,) * 3,
        scratch_shapes=[pltpu.VMEM(sums_type.shape, jnp.float32)],
        compiler_params=params,
        cost_estimate=cost,
        name="there_forces",
    )(lists, splat, sums, *parts)
    returned = swap(there, "group", 2)
    mine, other = pl.pallas_call(
        here_kernel,
        out_shape=(block_type, block_type),
        in_specs=[vmem] + [vmem] * 4,
        out_specs=(vmem,) * 2,
        scratch_shapes=[
            pltpu.VMEM(sums_type.shape, jnp.float32),
            pltpu.VMEM(flat_type.shape, jnp.float32),
        ],
        compiler_params=params,
        cost_estimate=cost,
        name="here_forces",
    )(lists, splat, sums, stars, flat)
    total = mine + returned[:8] + swap(other + returned[8:], "group", 1)
    live = lax.broadcasted_iota(jnp.int32, (1, slots), 1) < packed[1:2]
    output = jnp.where(live, total[:6], 0.0)
    return output[None, None]


def solution(mesh):
    return jax.shard_map(
        on_device,
        mesh=mesh,
        in_specs=(
            P(None, "blk"),
            P(None, "blk"),
            P(None, "blk"),
            P(None, "blk"),
            P("blk"),
            P("blk"),
            P("blk", "group", None),
            P("blk", "group"),
        ),
        out_specs=P("blk", "group", None, None),
        check_vma=False,
    )
```

```python
import functools

import jax
import jax.numpy as jnp
from jax import lax
from jax.experimental import pallas as pl
from jax.experimental.pallas import tpu as pltpu
from jax.sharding import PartitionSpec as P

LANES = 128
LANE_BITS = 7
SOFTEN = 0.01
VMEM_LIMIT = 48 * 1024 * 1024
SPREAD = 32
SHARERS = 4
SENT = 7


def predict_chunk(pos, vel, acc, jerk, mass, delta, chunk, total_stars):
    lanes = pl.ds(pl.multiple_of(chunk * LANES, LANES), LANES)
    step = delta[pl.ds(chunk, 1), :]
    p, v, a, j = pos[:, lanes], vel[:, lanes], acc[:, lanes], jerk[:, lanes]
    ppos = p + step * (v + step * (0.5 * a + step * (j / 6.0)))
    pvel = v + step * (a + step * (0.5 * j))
    weight = mass[pl.ds(chunk, 1), :] / total_stars
    return jnp.concatenate([ppos, pvel, weight, weight], 0)


def predict_kernel(total_stars, *refs):
    raw, count, (full, part, half, packed) = refs[:7], refs[7], refs[8:12]
    held, sems = refs[12:19], refs[19]
    copies = [
        pltpu.make_async_copy(source, target, sems.at[i])
        for i, (source, target) in enumerate(zip(raw, held))
    ]
    for copy in copies:
        copy.start()
    for copy in copies:
        copy.wait()

    def one(c, _):
        state = predict_chunk(*held[:6], c, total_stars)
        full[pl.ds(pl.multiple_of(c * 8, 8), 8), :] = state
        return _

    lax.fori_loop(0, full.shape[0] // 8, one, 0, unroll=8)
    for out in (part, half):
        size = out.shape[0] // SENT
        base = lax.rem(lax.axis_index("group"), full.shape[0] // (8 * size)) * size
        for c in range(size):
            state = full[pl.ds(pl.multiple_of((base + c) * 8, 8), 8), :]
            out[c * SENT : (c + 1) * SENT, :] = state[:SENT]
    packed[...] = jnp.zeros_like(packed)
    packed[0:1, :] = held[6][...]
    packed[1:2, :] = jnp.full((1, LANES), count[0, 0], jnp.int32)


def pair_terms(rows, stars, base, total):
    star = [stars[pl.ds(base + i, 1), :] for i in range(7)]
    dx, dy, dz, ux, uy, uz = (star[i] - rows[i] for i in range(6))
    inverse = lax.rsqrt(dx * dx + dy * dy + dz * dz + SOFTEN)
    square = inverse * inverse
    cube = (star[6] * inverse) * square
    radial = (dx * ux + dy * uy + dz * uz) * square
    ax, ay, az = dx * cube, dy * cube, dz * cube
    terms = (ax, ay, az, ux * cube, uy * cube, uz * cube, radial * ax, radial * ay, radial * az)
    return tuple(t + x for t, x in zip(total, terms))


def gather(lists, full, splat):
    slots = lists.shape[1]
    width = SHARERS * slots
    lane = lax.broadcasted_iota(jnp.int32, (8, width), 1)
    whole, base = None, 0
    for i in range(SHARERS):
        index = jnp.broadcast_to(lists[2 * i : 2 * i + 1, :], (8, slots))
        wide = jnp.concatenate([index] * SHARERS, 1)
        whole = jnp.where(lane >= base, pltpu.roll(wide, base, 1), whole) if i else wide
        base = base + lists[2 * i + 1, 0]
    for block in range(SHARERS):

        @pl.when(base > block * slots)
        def _():
            index = whole[:, block * slots : (block + 1) * slots]
            place = index & (LANES - 1)
            chunk = lax.shift_right_logical(index, LANE_BITS)

            def look(c, found):
                state = full[pl.ds(pl.multiple_of(c * 8, 8), 8), :]
                here = jnp.take_along_axis(state, place, axis=1, mode="promise_in_bounds")
                return jnp.where(chunk == c, here, found)

            found = lax.fori_loop(
                0, full.shape[0] // 8, look, jnp.zeros((8, slots), jnp.float32), unroll=16
            )
            for piece in range(0, slots, SPREAD):

                @pl.when(base > block * slots + piece)
                def _():
                    for row in range(piece, piece + SPREAD):
                        first = (block * slots + row) * 8
                        splat[first : first + 8, :] = jnp.broadcast_to(
                            found[:, row : row + 1], (8, LANES)
                        )


def group_bounds(lists):
    counts = [lists[2 * owner + 1, 0] for owner in range(SHARERS)]
    there, here = counts[0] + counts[1], counts[2] + counts[3]
    return (jnp.maximum(there, here) + 7) // 8, (there + here + 7) // 8


def add_lanes(begin, end, sums, flat):
    slots = flat.shape[1] // SHARERS
    for block in range(SHARERS):

        @pl.when((end * 8 > block * slots) & (begin * 8 < (block + 1) * slots))
        def _():
            part = pl.ds(block * slots, slots)
            for j in range(6):
                flat[pl.ds(j, 1), part] = jnp.sum(sums[j, part, :], axis=1)[None, :]


def cut(lists, owner, flat, slots):
    first = sum(lists[2 * before + 1, 0] for before in range(owner))
    return pltpu.roll(flat, flat.shape[1] - first, 1)[:, :slots] if owner else flat[:, :slots]


def add_forces(begin, end, splat, stars, chunks, stride, unroll, before, after, height=8):
    def group(g, _):
        place = pl.multiple_of(g * height, 8)
        rows = [
            jnp.concatenate(
                [splat[pl.ds((place + k) * 8 + i, 8, stride=8), :] for k in range(0, height, 8)], 0
            )
            for i in range(6)
        ]
        zero = jnp.zeros((height, LANES), jnp.float32)
        if before is None:
            total = (zero,) * 9
        else:
            total = tuple(before[i, pl.ds(place, height), :] for i in range(6)) + (zero,) * 3
        total = lax.fori_loop(
            0,
            chunks[1],
            lambda c, t: pair_terms(rows, stars, (chunks[0] + c) * stride, t),
            total,
            unroll=unroll,
        )
        for i in range(3):
            after[i, pl.ds(place, height), :] = total[i]
            after[3 + i, pl.ds(place, height), :] = total[3 + i] - 3.0 * total[6 + i]
        return _

    lax.fori_loop(begin, end, group, 0)


def near_kernel(lists, full, splat, sums):
    gather(lists, full, splat)
    _, groups = group_bounds(lists)
    size = full.shape[0] // (8 * SHARERS)
    own = (lax.rem(lax.axis_index("group"), SHARERS) * size, size)
    add_forces(0, (groups + 1) // 2, splat, full, own, 8, size, None, sums, 16)


def there_kernel(*refs):
    lists, splat, sums = refs[:3]
    parts, (blocks, flat, stars, held) = refs[3:-4], refs[-4:]
    begin = 0
    for part in parts:
        stars[pl.ds(begin, part.shape[0]), :] = part[...]
        begin += part.shape[0]
    shared, _ = group_bounds(lists)
    far = (0, stars.shape[0] // SENT)
    add_forces(0, shared, splat, stars, far, SENT, 48, sums, held)
    add_lanes(0, shared, held, flat)
    for owner in range(2):
        blocks[owner * 8 : owner * 8 + 8, :] = cut(lists, owner, flat[...], blocks.shape[1])


def here_kernel(lists, splat, sums, stars, flat, mine, other, held, rest):
    shared, groups = group_bounds(lists)
    far = (0, stars.shape[0] // SENT)
    add_forces(shared, groups, splat, stars, far, SENT, 48, sums, held)
    add_lanes(shared, groups, held, rest)
    done = lax.broadcasted_iota(jnp.int32, flat.shape, 1) < shared * 8
    whole = jnp.where(done, flat[...], rest[...])
    for owner, out in ((2, mine), (3, other)):
        out[...] = cut(lists, owner, whole, out.shape[1])


def on_device(
    star_pos, star_vel, star_acc, star_jerk, star_mass, star_dt, active_list, active_count
):
    n_blk = lax.axis_size("blk")
    n_group = lax.axis_size("group")
    shard = star_mass.shape[0]
    total_stars = shard * n_blk
    slots = active_list.shape[2]
    chunks = shard // LANES
    room = SHARERS * slots
    vmem = pl.BlockSpec(memory_space=pltpu.VMEM)
    smem = pl.BlockSpec(memory_space=pltpu.SMEM)
    params = pltpu.CompilerParams(vmem_limit_bytes=VMEM_LIMIT)
    splat_type = jax.ShapeDtypeStruct((room * 8, LANES), jnp.float32)
    sums_type = jax.ShapeDtypeStruct((6, room, LANES), jnp.float32)
    raw = (
        star_pos,
        star_vel,
        star_acc,
        star_jerk,
        star_mass.reshape(chunks, LANES),
        star_dt.reshape(chunks, LANES),
        active_list[0],
    )

    def swap(x, axis, bits):
        return lax.ppermute(x, axis, [(i, i ^ bits) for i in range(lax.axis_size(axis))])

    def trade(x, step):
        pairs = [
            (b * n_group + g, (b ^ step ^ (2 if g & 2 else 1)) * n_group + g)
            for b in range(n_blk)
            for g in range(n_group)
        ]
        return lax.ppermute(x, ("blk", "group"), pairs)

    part_type = jax.ShapeDtypeStruct((chunks * SENT // SHARERS, LANES), jnp.float32)
    full, part, half, packed = pl.pallas_call(
        functools.partial(predict_kernel, total_stars),
        out_shape=(
            jax.ShapeDtypeStruct((chunks * 8, LANES), jnp.float32),
            part_type,
            jax.ShapeDtypeStruct((chunks * SENT // 2, LANES), jnp.float32),
            jax.ShapeDtypeStruct((8, slots), jnp.int32),
        ),
        in_specs=[pl.BlockSpec(memory_space=pltpu.HBM)] * 7 + [smem],
        out_specs=(vmem,) * 4,
        scratch_shapes=[pltpu.VMEM(x.shape, x.dtype) for x in raw]
        + [pltpu.SemaphoreType.DMA((7,))],
        compiler_params=params,
        name="predict",
    )(*(pltpu.with_memory_space_constraint(x, pltpu.HBM) for x in raw), active_count)
    parts = []
    for step in range(0, n_blk, 4):
        parts.append(trade(half, step))
        parts += [swap(part, "blk", bits) for bits in (step + 3, step) if bits]
    core, *others = (swap(packed, "group", bits) for bits in range(1, SHARERS))
    lists = jnp.concatenate([x[:2] for x in (*others, packed, core)], 0)
    splat, sums = pl.pallas_call(
        near_kernel,
        out_shape=(splat_type, sums_type),
        in_specs=[vmem] * 2,
        out_specs=(vmem,) * 2,
        compiler_params=params,
        name="near_forces",
    )(lists, full)
    block_type = jax.ShapeDtypeStruct((8, slots), jnp.float32)
    pairs = slots * shard
    cost = pl.CostEstimate(flops=40 * pairs, bytes_accessed=pairs, transcendentals=pairs)
    flat_type = jax.ShapeDtypeStruct((8, SHARERS * slots), jnp.float32)
    stars_type = jax.ShapeDtypeStruct((sum(x.shape[0] for x in parts), LANES), jnp.float32)
    there, flat, stars = pl.pallas_call(
        there_kernel,
        out_shape=(
            jax.ShapeDtypeStruct((16, slots), jnp.float32),
            flat_type,
            stars_type,
        ),
        in_specs=[vmem] * (3 + len(parts)),
        out_specs=(vmem,) * 3,
        scratch_shapes=[pltpu.VMEM(sums_type.shape, jnp.float32)],
        compiler_params=params,
        cost_estimate=cost,
        name="there_forces",
    )(lists, splat, sums, *parts)
    returned = swap(there, "group", 2)
    mine, other = pl.pallas_call(
        here_kernel,
        out_shape=(block_type, block_type),
        in_specs=[vmem] * 5,
        out_specs=(vmem,) * 2,
        scratch_shapes=[
            pltpu.VMEM(sums_type.shape, jnp.float32),
            pltpu.VMEM(flat_type.shape, jnp.float32),
        ],
        compiler_params=params,
        cost_estimate=cost,
        name="here_forces",
    )(lists, splat, sums, stars, flat)
    total = mine + returned[:8] + swap(other + returned[8:], "group", 1)
    live = lax.broadcasted_iota(jnp.int32, (1, slots), 1) < packed[1:2]
    output = jnp.where(live, total[:6], 0.0)
    return output[None, None]


def solution(mesh):
    return jax.shard_map(
        on_device,
        mesh=mesh,
        in_specs=(
            P(None, "blk"),
            P(None, "blk"),
            P(None, "blk"),
            P(None, "blk"),
            P("blk"),
            P("blk"),
            P("blk", "group", None),
            P("blk", "group"),
        ),
        out_specs=P("blk", "group", None, None),
        check_vma=False,
    )
```

```python
import functools

import jax
import jax.numpy as jnp
from jax import lax
from jax.experimental import pallas as pl
from jax.experimental.pallas import tpu as pltpu
from jax.sharding import PartitionSpec as P

LANES = 128
LANE_BITS = 7
SOFTEN = 0.01
VMEM_LIMIT = 48 * 1024 * 1024
SPREAD = 32
SHARERS = 4
SENT = 7
LEAN = 4


def predict_chunk(pos, vel, acc, jerk, mass, delta, chunk, total_stars):
    lanes = pl.ds(pl.multiple_of(chunk * LANES, LANES), LANES)
    step = delta[pl.ds(chunk, 1), :]
    p, v, a, j = pos[:, lanes], vel[:, lanes], acc[:, lanes], jerk[:, lanes]
    ppos = p + step * (v + step * (0.5 * a + step * (j / 6.0)))
    pvel = v + step * (a + step * (0.5 * j))
    weight = mass[pl.ds(chunk, 1), :] / total_stars
    return jnp.concatenate([ppos, pvel, weight, weight], 0)


def predict_kernel(total_stars, *refs):
    raw, count, (full, part, half, packed) = refs[:7], refs[7], refs[8:12]
    held, sems = refs[12:19], refs[19]
    copies = [
        pltpu.make_async_copy(source, target, sems.at[i])
        for i, (source, target) in enumerate(zip(raw, held))
    ]
    for copy in copies:
        copy.start()
    for copy in copies:
        copy.wait()

    def one(c, _):
        state = predict_chunk(*held[:6], c, total_stars)
        full[pl.ds(pl.multiple_of(c * 8, 8), 8), :] = state
        return _

    lax.fori_loop(0, full.shape[0] // 8, one, 0, unroll=8)
    for out in (part, half):
        size = out.shape[0] // SENT
        base = lax.rem(lax.axis_index("group"), full.shape[0] // (8 * size)) * size
        for c in range(size):
            state = full[pl.ds(pl.multiple_of((base + c) * 8, 8), 8), :]
            out[c * SENT : (c + 1) * SENT, :] = state[:SENT]
    packed[...] = jnp.zeros_like(packed)
    packed[0:1, :] = held[6][...]
    packed[1:2, :] = jnp.full((1, LANES), count[0, 0], jnp.int32)


def pair_terms(rows, stars, base, total):
    star = [stars[pl.ds(base + i, 1), :] for i in range(7)]
    dx, dy, dz, ux, uy, uz = (star[i] - rows[i] for i in range(6))
    inverse = lax.rsqrt(dx * dx + dy * dy + dz * dz + SOFTEN)
    square = inverse * inverse
    cube = (star[6] * inverse) * square
    radial = (dx * ux + dy * uy + dz * uz) * square
    ax, ay, az = dx * cube, dy * cube, dz * cube
    terms = (ax, ay, az, ux * cube, uy * cube, uz * cube, radial * ax, radial * ay, radial * az)
    return tuple(t + x for t, x in zip(total, terms))


def gather(lists, full, splat):
    slots = lists.shape[1]
    width = SHARERS * slots
    lane = lax.broadcasted_iota(jnp.int32, (8, width), 1)
    whole, base = None, 0
    for i in range(SHARERS):
        index = jnp.broadcast_to(lists[2 * i : 2 * i + 1, :], (8, slots))
        wide = jnp.concatenate([index] * SHARERS, 1)
        whole = jnp.where(lane >= base, pltpu.roll(wide, base, 1), whole) if i else wide
        base = base + lists[2 * i + 1, 0]
    for block in range(SHARERS):

        @pl.when(base > block * slots)
        def _():
            index = whole[:, block * slots : (block + 1) * slots]
            place = index & (LANES - 1)
            chunk = lax.shift_right_logical(index, LANE_BITS)

            def look(c, found):
                state = full[pl.ds(pl.multiple_of(c * 8, 8), 8), :]
                here = jnp.take_along_axis(state, place, axis=1, mode="promise_in_bounds")
                return jnp.where(chunk == c, here, found)

            found = lax.fori_loop(
                0, full.shape[0] // 8, look, jnp.zeros((8, slots), jnp.float32), unroll=16
            )
            for piece in range(0, slots, SPREAD):

                @pl.when(base > block * slots + piece)
                def _():
                    for row in range(piece, piece + SPREAD):
                        first = (block * slots + row) * 8
                        splat[first : first + 8, :] = jnp.broadcast_to(
                            found[:, row : row + 1], (8, LANES)
                        )


def group_bounds(lists):
    counts = [lists[2 * owner + 1, 0] for owner in range(SHARERS)]
    there, here = counts[0] + counts[1], counts[2] + counts[3]
    return (jnp.maximum(there, here) + 7) // 8, (there + here + 7) // 8


def add_lanes(begin, end, sums, flat):
    slots = flat.shape[1] // SHARERS
    for block in range(SHARERS):

        @pl.when((end * 8 > block * slots) & (begin * 8 < (block + 1) * slots))
        def _():
            part = pl.ds(block * slots, slots)
            for j in range(6):
                flat[pl.ds(j, 1), part] = jnp.sum(sums[j, part, :], axis=1)[None, :]


def cut(lists, owner, flat, slots):
    first = sum(lists[2 * before + 1, 0] for before in range(owner))
    return pltpu.roll(flat, flat.shape[1] - first, 1)[:, :slots] if owner else flat[:, :slots]


def add_forces(begin, end, splat, stars, chunks, stride, unroll, before, after, height=8):
    def group(g, _):
        place = pl.multiple_of(g * height, 8)
        rows = [
            jnp.concatenate(
                [splat[pl.ds((place + k) * 8 + i, 8, stride=8), :] for k in range(0, height, 8)], 0
            )
            for i in range(6)
        ]
        zero = jnp.zeros((height, LANES), jnp.float32)
        if before is None:
            total = (zero,) * 9
        else:
            total = tuple(before[i, pl.ds(place, height), :] for i in range(6)) + (zero,) * 3
        total = lax.fori_loop(
            0,
            chunks[1],
            lambda c, t: pair_terms(rows, stars, (chunks[0] + c) * stride, t),
            total,
            unroll=unroll,
        )
        for i in range(3):
            after[i, pl.ds(place, height), :] = total[i]
            after[3 + i, pl.ds(place, height), :] = total[3 + i] - 3.0 * total[6 + i]
        return _

    lax.fori_loop(begin, end, group, 0)


def near_kernel(lists, full, splat, sums):
    gather(lists, full, splat)
    _, groups = group_bounds(lists)
    size = full.shape[0] // (8 * SHARERS)
    place = lax.rem(lax.axis_index("group"), SHARERS)
    odd = lax.rem(place, 2)
    groups = (groups + 1) // 2
    first, less, more = place * size - odd * LEAN, size - LEAN, 2 * LEAN
    add_forces(0, groups, splat, full, (first, less), 8, less, None, sums, 16)
    add_forces(0, groups * odd, splat, full, (first + less, more), 8, more, sums, sums, 16)


def there_kernel(*refs):
    lists, splat, sums = refs[:3]
    parts, (blocks, flat, stars, held) = refs[3:-4], refs[-4:]
    begin = 0
    for part in parts:
        stars[pl.ds(begin, part.shape[0]), :] = part[...]
        begin += part.shape[0]
    shared, _ = group_bounds(lists)
    far = (0, stars.shape[0] // SENT)
    add_forces(0, shared, splat, stars, far, SENT, 48, sums, held)
    add_lanes(0, shared, held, flat)
    for owner in range(2):
        blocks[owner * 8 : owner * 8 + 8, :] = cut(lists, owner, flat[...], blocks.shape[1])


def here_kernel(lists, splat, sums, stars, flat, mine, other, held, rest):
    shared, groups = group_bounds(lists)
    far = (0, stars.shape[0] // SENT)
    add_forces(shared, groups, splat, stars, far, SENT, 48, sums, held)
    add_lanes(shared, groups, held, rest)
    done = lax.broadcasted_iota(jnp.int32, flat.shape, 1) < shared * 8
    whole = jnp.where(done, flat[...], rest[...])
    for owner, out in ((2, mine), (3, other)):
        out[...] = cut(lists, owner, whole, out.shape[1])


def on_device(
    star_pos, star_vel, star_acc, star_jerk, star_mass, star_dt, active_list, active_count
):
    n_blk = lax.axis_size("blk")
    n_group = lax.axis_size("group")
    shard = star_mass.shape[0]
    total_stars = shard * n_blk
    slots = active_list.shape[2]
    chunks = shard // LANES
    room = SHARERS * slots
    vmem = pl.BlockSpec(memory_space=pltpu.VMEM)
    smem = pl.BlockSpec(memory_space=pltpu.SMEM)
    params = pltpu.CompilerParams(vmem_limit_bytes=VMEM_LIMIT)
    splat_type = jax.ShapeDtypeStruct((room * 8, LANES), jnp.float32)
    sums_type = jax.ShapeDtypeStruct((6, room, LANES), jnp.float32)
    raw = (
        star_pos,
        star_vel,
        star_acc,
        star_jerk,
        star_mass.reshape(chunks, LANES),
        star_dt.reshape(chunks, LANES),
        active_list[0],
    )

    def swap(x, axis, bits):
        return lax.ppermute(x, axis, [(i, i ^ bits) for i in range(lax.axis_size(axis))])

    def trade(x, step):
        pairs = [
            (b * n_group + g, (b ^ step ^ (2 if g & 2 else 1)) * n_group + g)
            for b in range(n_blk)
            for g in range(n_group)
        ]
        return lax.ppermute(x, ("blk", "group"), pairs)

    part_type = jax.ShapeDtypeStruct((chunks * SENT // SHARERS, LANES), jnp.float32)
    full, part, half, packed = pl.pallas_call(
        functools.partial(predict_kernel, total_stars),
        out_shape=(
            jax.ShapeDtypeStruct((chunks * 8, LANES), jnp.float32),
            part_type,
            jax.ShapeDtypeStruct((chunks * SENT // 2, LANES), jnp.float32),
            jax.ShapeDtypeStruct((8, slots), jnp.int32),
        ),
        in_specs=[pl.BlockSpec(memory_space=pltpu.HBM)] * 7 + [smem],
        out_specs=(vmem,) * 4,
        scratch_shapes=[pltpu.VMEM(x.shape, x.dtype) for x in raw]
        + [pltpu.SemaphoreType.DMA((7,))],
        compiler_params=params,
        name="predict",
    )(*(pltpu.with_memory_space_constraint(x, pltpu.HBM) for x in raw), active_count)
    parts = []
    for step in range(0, n_blk, 4):
        parts.append(trade(half, step))
        parts += [swap(part, "blk", bits) for bits in (step + 3, step) if bits]
    core, *others = (swap(packed, "group", bits) for bits in range(1, SHARERS))
    lists = jnp.concatenate([x[:2] for x in (*others, packed, core)], 0)
    splat, sums = pl.pallas_call(
        near_kernel,
        out_shape=(splat_type, sums_type),
        in_specs=[vmem] * 2,
        out_specs=(vmem,) * 2,
        compiler_params=params,
        name="near_forces",
    )(lists, full)
    block_type = jax.ShapeDtypeStruct((8, slots), jnp.float32)
    pairs = slots * shard
    cost = pl.CostEstimate(flops=40 * pairs, bytes_accessed=pairs, transcendentals=pairs)
    flat_type = jax.ShapeDtypeStruct((8, SHARERS * slots), jnp.float32)
    stars_type = jax.ShapeDtypeStruct((sum(x.shape[0] for x in parts), LANES), jnp.float32)
    there, flat, stars = pl.pallas_call(
        there_kernel,
        out_shape=(
            jax.ShapeDtypeStruct((16, slots), jnp.float32),
            flat_type,
            stars_type,
        ),
        in_specs=[vmem] * (3 + len(parts)),
        out_specs=(vmem,) * 3,
        scratch_shapes=[pltpu.VMEM(sums_type.shape, jnp.float32)],
        compiler_params=params,
        cost_estimate=cost,
        name="there_forces",
    )(lists, splat, sums, *parts)
    returned = swap(there, "group", 2)
    mine, other = pl.pallas_call(
        here_kernel,
        out_shape=(block_type, block_type),
        in_specs=[vmem] * 5,
        out_specs=(vmem,) * 2,
        scratch_shapes=[
            pltpu.VMEM(sums_type.shape, jnp.float32),
            pltpu.VMEM(flat_type.shape, jnp.float32),
        ],
        compiler_params=params,
        cost_estimate=cost,
        name="here_forces",
    )(lists, splat, sums, stars, flat)
    total = mine + returned[:8] + swap(other + returned[8:], "group", 1)
    live = lax.broadcasted_iota(jnp.int32, (1, slots), 1) < packed[1:2]
    output = jnp.where(live, total[:6], 0.0)
    return output[None, None]


def solution(mesh):
    return jax.shard_map(
        on_device,
        mesh=mesh,
        in_specs=(
            P(None, "blk"),
            P(None, "blk"),
            P(None, "blk"),
            P(None, "blk"),
            P("blk"),
            P("blk"),
            P("blk", "group", None),
            P("blk", "group"),
        ),
        out_specs=P("blk", "group", None, None),
        check_vma=False,
    )
```

```python
import functools

import jax
import jax.numpy as jnp
from jax import lax
from jax.experimental import pallas as pl
from jax.experimental.pallas import tpu as pltpu
from jax.sharding import PartitionSpec as P

LANES = 128
LANE_BITS = 7
SOFTEN = 0.01
VMEM_LIMIT = 48 * 1024 * 1024
SPREAD = 32
SHARERS = 4
SENT = 7
LEAN = 4
PAIR = 2


def predict_chunk(pos, vel, acc, jerk, mass, delta, chunk, total_stars):
    lanes = pl.ds(pl.multiple_of(chunk * LANES, LANES), LANES)
    step = delta[pl.ds(chunk, 1), :]
    p, v, a, j = pos[:, lanes], vel[:, lanes], acc[:, lanes], jerk[:, lanes]
    ppos = p + step * (v + step * (0.5 * a + step * (j / 6.0)))
    pvel = v + step * (a + step * (0.5 * j))
    weight = mass[pl.ds(chunk, 1), :] / total_stars
    return jnp.concatenate([ppos, pvel, weight, weight], 0)


def predict_kernel(total_stars, *refs):
    raw, count, (full, part, half, packed) = refs[:7], refs[7], refs[8:12]
    held, sems = refs[12:19], refs[19]
    copies = [
        pltpu.make_async_copy(source, target, sems.at[i])
        for i, (source, target) in enumerate(zip(raw, held))
    ]
    for copy in copies:
        copy.start()
    for copy in copies:
        copy.wait()

    def one(c, _):
        state = predict_chunk(*held[:6], c, total_stars)
        full[pl.ds(pl.multiple_of(c * 8, 8), 8), :] = state
        return _

    lax.fori_loop(0, full.shape[0] // 8, one, 0, unroll=8)
    for out in (part, half):
        size = out.shape[0] // SENT
        base = lax.rem(lax.axis_index("group"), full.shape[0] // (8 * size)) * size
        for c in range(size):
            state = full[pl.ds(pl.multiple_of((base + c) * 8, 8), 8), :]
            out[c * SENT : (c + 1) * SENT, :] = state[:SENT]
    packed[...] = jnp.zeros_like(packed)
    packed[0:1, :] = held[6][...]
    packed[1:2, :] = jnp.full((1, LANES), count[0, 0], jnp.int32)


def pair_terms(rows, stars, base, total):
    star = [stars[pl.ds(base + i, 1), :] for i in range(7)]
    dx, dy, dz, ux, uy, uz = (star[i] - rows[i] for i in range(6))
    inverse = lax.rsqrt(dx * dx + dy * dy + dz * dz + SOFTEN)
    square = inverse * inverse
    cube = (star[6] * inverse) * square
    radial = (dx * ux + dy * uy + dz * uz) * square
    ax, ay, az = dx * cube, dy * cube, dz * cube
    terms = (ax, ay, az, ux * cube, uy * cube, uz * cube, radial * ax, radial * ay, radial * az)
    return tuple(t + x for t, x in zip(total, terms))


def gather(lists, full, splat):
    slots = lists.shape[1]
    width = PAIR * slots
    lane = lax.broadcasted_iota(jnp.int32, (8, width), 1)
    whole, base = None, 0
    for i in range(PAIR):
        index = jnp.broadcast_to(lists[2 * i : 2 * i + 1, :], (8, slots))
        wide = jnp.concatenate([index] * PAIR, 1)
        whole = jnp.where(lane >= base, pltpu.roll(wide, base, 1), whole) if i else wide
        base = base + lists[2 * i + 1, 0]
    for block in range(PAIR):

        @pl.when(base > block * slots)
        def _():
            index = whole[:, block * slots : (block + 1) * slots]
            place = index & (LANES - 1)
            chunk = lax.shift_right_logical(index, LANE_BITS)

            def look(c, found):
                state = full[pl.ds(pl.multiple_of(c * 8, 8), 8), :]
                here = jnp.take_along_axis(state, place, axis=1, mode="promise_in_bounds")
                return jnp.where(chunk == c, here, found)

            found = lax.fori_loop(
                0, full.shape[0] // 8, look, jnp.zeros((8, slots), jnp.float32), unroll=16
            )
            for piece in range(0, slots, SPREAD):

                @pl.when(base > block * slots + piece)
                def _():
                    for row in range(piece, piece + SPREAD):
                        first = (block * slots + row) * 8
                        splat[first : first + 8, :] = jnp.broadcast_to(
                            found[:, row : row + 1], (8, LANES)
                        )


def group_count(lists):
    return (lists[1, 0] + lists[3, 0] + 7) // 8


def add_lanes(begin, end, sums, flat):
    slots = flat.shape[1] // PAIR
    for block in range(PAIR):

        @pl.when((end * 8 > block * slots) & (begin * 8 < (block + 1) * slots))
        def _():
            part = pl.ds(block * slots, slots)
            for j in range(6):
                flat[pl.ds(j, 1), part] = jnp.sum(sums[j, part, :], axis=1)[None, :]


def cut(lists, owner, flat, slots):
    first = sum(lists[2 * before + 1, 0] for before in range(owner))
    return pltpu.roll(flat, flat.shape[1] - first, 1)[:, :slots] if owner else flat[:, :slots]


def add_forces(begin, end, splat, stars, chunks, stride, unroll, before, after, height=8):
    def group(g, _):
        place = pl.multiple_of(g * height, 8)
        rows = [
            jnp.concatenate(
                [splat[pl.ds((place + k) * 8 + i, 8, stride=8), :] for k in range(0, height, 8)], 0
            )
            for i in range(6)
        ]
        zero = jnp.zeros((height, LANES), jnp.float32)
        if before is None:
            total = (zero,) * 9
        else:
            total = tuple(before[i, pl.ds(place, height), :] for i in range(6)) + (zero,) * 3
        total = lax.fori_loop(
            0,
            chunks[1],
            lambda c, t: pair_terms(rows, stars, (chunks[0] + c) * stride, t),
            total,
            unroll=unroll,
        )
        for i in range(3):
            after[i, pl.ds(place, height), :] = total[i]
            after[3 + i, pl.ds(place, height), :] = total[3 + i] - 3.0 * total[6 + i]
        return _

    lax.fori_loop(begin, end, group, 0)


def near_kernel(lists, full, splat, sums):
    gather(lists, full, splat)
    groups = group_count(lists)
    size = full.shape[0] // (8 * SHARERS)
    place = lax.rem(lax.axis_index("group"), SHARERS)
    odd = lax.rem(place, 2)
    groups = (groups + 1) // 2
    first, less, more = place * size - odd * LEAN, size - LEAN, 2 * LEAN
    add_forces(0, groups, splat, full, (first, less), 8, less, None, sums, 16)
    add_forces(0, groups * odd, splat, full, (first + less, more), 8, more, sums, sums, 16)


def there_kernel(*refs):
    others, lists, splat, sums, own_splat, own_sums = refs[:6]
    parts, (blocks, flat, stars, held, own_held, wide) = refs[6:-6], refs[-6:]
    begin = 0
    for part in parts:
        stars[pl.ds(begin, part.shape[0]), :] = part[...]
        begin += part.shape[0]
    far = (0, stars.shape[0] // SENT)
    there = group_count(others)
    shared = jnp.maximum(group_count(lists) - there, 0)
    add_forces(0, there, splat, stars, far, SENT, 48, sums, held)
    add_forces(0, shared, own_splat, stars, far, SENT, 48, own_sums, own_held)
    add_lanes(0, there, held, wide)
    add_lanes(0, shared, own_held, flat)
    for owner in range(PAIR):
        blocks[owner * 8 : owner * 8 + 8, :] = cut(others, owner, wide[...], blocks.shape[1])


def here_kernel(others, lists, splat, sums, stars, flat, mine, other, held, rest):
    groups = group_count(lists)
    shared = jnp.maximum(groups - group_count(others), 0)
    far = (0, stars.shape[0] // SENT)
    add_forces(shared, groups, splat, stars, far, SENT, 48, sums, held)
    add_lanes(shared, groups, held, rest)
    done = lax.broadcasted_iota(jnp.int32, flat.shape, 1) < shared * 8
    whole = jnp.where(done, flat[...], rest[...])
    for owner, out in enumerate((mine, other)):
        out[...] = cut(lists, owner, whole, out.shape[1])


def on_device(
    star_pos, star_vel, star_acc, star_jerk, star_mass, star_dt, active_list, active_count
):
    n_blk = lax.axis_size("blk")
    n_group = lax.axis_size("group")
    shard = star_mass.shape[0]
    total_stars = shard * n_blk
    slots = active_list.shape[2]
    chunks = shard // LANES
    room = PAIR * slots
    vmem = pl.BlockSpec(memory_space=pltpu.VMEM)
    smem = pl.BlockSpec(memory_space=pltpu.SMEM)
    params = pltpu.CompilerParams(vmem_limit_bytes=VMEM_LIMIT)
    splat_type = jax.ShapeDtypeStruct((room * 8, LANES), jnp.float32)
    sums_type = jax.ShapeDtypeStruct((6, room, LANES), jnp.float32)
    raw = (
        star_pos,
        star_vel,
        star_acc,
        star_jerk,
        star_mass.reshape(chunks, LANES),
        star_dt.reshape(chunks, LANES),
        active_list[0],
    )

    def swap(x, axis, bits):
        return lax.ppermute(x, axis, [(i, i ^ bits) for i in range(lax.axis_size(axis))])

    def trade(x, step):
        pairs = [
            (b * n_group + g, (b ^ step ^ (2 if g & 2 else 1)) * n_group + g)
            for b in range(n_blk)
            for g in range(n_group)
        ]
        return lax.ppermute(x, ("blk", "group"), pairs)

    part_type = jax.ShapeDtypeStruct((chunks * SENT // SHARERS, LANES), jnp.float32)
    full, part, half, packed = pl.pallas_call(
        functools.partial(predict_kernel, total_stars),
        out_shape=(
            jax.ShapeDtypeStruct((chunks * 8, LANES), jnp.float32),
            part_type,
            jax.ShapeDtypeStruct((chunks * SENT // 2, LANES), jnp.float32),
            jax.ShapeDtypeStruct((8, slots), jnp.int32),
        ),
        in_specs=[pl.BlockSpec(memory_space=pltpu.HBM)] * 7 + [smem],
        out_specs=(vmem,) * 4,
        scratch_shapes=[pltpu.VMEM(x.shape, x.dtype) for x in raw]
        + [pltpu.SemaphoreType.DMA((7,))],
        compiler_params=params,
        name="predict",
    )(*(pltpu.with_memory_space_constraint(x, pltpu.HBM) for x in raw), active_count)
    parts = []
    for step in range(0, n_blk, 4):
        parts.append(trade(half, step))
        parts += [swap(part, "blk", bits) for bits in (step + 3, step) if bits]
    core, *others = (swap(packed, "group", bits) for bits in range(1, SHARERS))
    lists = jnp.concatenate([packed[:2], core[:2]], 0)

    def near(x, name):
        return pl.pallas_call(
            near_kernel,
            out_shape=(splat_type, sums_type),
            in_specs=[vmem] * 2,
            out_specs=(vmem,) * 2,
            compiler_params=params,
            name=name,
        )(x, full)

    own_splat, own_sums = near(lists, "near_own")
    own_sums, others = lax.optimization_barrier((own_sums, others))
    others = jnp.concatenate([x[:2] for x in others], 0)
    splat, sums = near(others, "near_other")
    block_type = jax.ShapeDtypeStruct((8, slots), jnp.float32)
    pairs = slots * shard
    cost = pl.CostEstimate(flops=40 * pairs, bytes_accessed=pairs, transcendentals=pairs)
    flat_type = jax.ShapeDtypeStruct((8, PAIR * slots), jnp.float32)
    stars_type = jax.ShapeDtypeStruct((sum(x.shape[0] for x in parts), LANES), jnp.float32)
    there, flat, stars = pl.pallas_call(
        there_kernel,
        out_shape=(
            jax.ShapeDtypeStruct((16, slots), jnp.float32),
            flat_type,
            stars_type,
        ),
        in_specs=[vmem] * (6 + len(parts)),
        out_specs=(vmem,) * 3,
        scratch_shapes=[pltpu.VMEM(sums_type.shape, jnp.float32)] * 2
        + [pltpu.VMEM(flat_type.shape, jnp.float32)],
        compiler_params=params,
        cost_estimate=cost,
        name="there_forces",
    )(others, lists, splat, sums, own_splat, own_sums, *parts)
    returned = swap(there, "group", 2)
    mine, other = pl.pallas_call(
        here_kernel,
        out_shape=(block_type, block_type),
        in_specs=[vmem] * 6,
        out_specs=(vmem,) * 2,
        scratch_shapes=[
            pltpu.VMEM(sums_type.shape, jnp.float32),
            pltpu.VMEM(flat_type.shape, jnp.float32),
        ],
        compiler_params=params,
        cost_estimate=cost,
        name="here_forces",
    )(others, lists, own_splat, own_sums, stars, flat)
    total = mine + returned[:8] + swap(other + returned[8:], "group", 1)
    live = lax.broadcasted_iota(jnp.int32, (1, slots), 1) < packed[1:2]
    output = jnp.where(live, total[:6], 0.0)
    return output[None, None]


def solution(mesh):
    return jax.shard_map(
        on_device,
        mesh=mesh,
        in_specs=(
            P(None, "blk"),
            P(None, "blk"),
            P(None, "blk"),
            P(None, "blk"),
            P("blk"),
            P("blk"),
            P("blk", "group", None),
            P("blk", "group"),
        ),
        out_specs=P("blk", "group", None, None),
        check_vma=False,
    )
```

```python
import functools

import jax
import jax.numpy as jnp
from jax import lax
from jax.experimental import pallas as pl
from jax.experimental.pallas import tpu as pltpu
from jax.sharding import PartitionSpec as P

LANES = 128
LANE_BITS = 7
SOFTEN = 0.01
VMEM_LIMIT = 48 * 1024 * 1024
SPREAD = 32
SHARERS = 4
SENT = 7
LEAN = 6


def predict_chunk(pos, vel, acc, jerk, mass, delta, chunk, total_stars):
    lanes = pl.ds(pl.multiple_of(chunk * LANES, LANES), LANES)
    step = delta[pl.ds(chunk, 1), :]
    p, v, a, j = pos[:, lanes], vel[:, lanes], acc[:, lanes], jerk[:, lanes]
    ppos = p + step * (v + step * (0.5 * a + step * (j / 6.0)))
    pvel = v + step * (a + step * (0.5 * j))
    weight = mass[pl.ds(chunk, 1), :] / total_stars
    return jnp.concatenate([ppos, pvel, weight, weight], 0)


def predict_kernel(total_stars, *refs):
    raw, count, (full, part, half, packed) = refs[:7], refs[7], refs[8:12]
    held, sems = refs[12:19], refs[19]
    copies = [
        pltpu.make_async_copy(source, target, sems.at[i])
        for i, (source, target) in enumerate(zip(raw, held))
    ]
    for copy in copies:
        copy.start()
    for copy in copies:
        copy.wait()

    def one(c, _):
        state = predict_chunk(*held[:6], c, total_stars)
        full[pl.ds(pl.multiple_of(c * 8, 8), 8), :] = state
        return _

    lax.fori_loop(0, full.shape[0] // 8, one, 0, unroll=8)
    for out in (part, half):
        size = out.shape[0] // SENT
        base = lax.rem(lax.axis_index("group"), full.shape[0] // (8 * size)) * size
        for c in range(size):
            state = full[pl.ds(pl.multiple_of((base + c) * 8, 8), 8), :]
            out[c * SENT : (c + 1) * SENT, :] = state[:SENT]
    packed[...] = jnp.zeros_like(packed)
    packed[0:1, :] = held[6][...]
    packed[1:2, :] = jnp.full((1, LANES), count[0, 0], jnp.int32)


def pair_terms(rows, stars, base, total):
    star = [stars[pl.ds(base + i, 1), :] for i in range(7)]
    dx, dy, dz, ux, uy, uz = (star[i] - rows[i] for i in range(6))
    inverse = lax.rsqrt(dx * dx + dy * dy + dz * dz + SOFTEN)
    square = inverse * inverse
    cube = (star[6] * inverse) * square
    radial = (dx * ux + dy * uy + dz * uz) * square
    ax, ay, az = dx * cube, dy * cube, dz * cube
    terms = (ax, ay, az, ux * cube, uy * cube, uz * cube, radial * ax, radial * ay, radial * az)
    return tuple(t + x for t, x in zip(total, terms))


def gather(lists, full, splat):
    slots = lists.shape[1]
    width = SHARERS * slots
    lane = lax.broadcasted_iota(jnp.int32, (8, width), 1)
    whole, base = None, 0
    for i in range(SHARERS):
        index = jnp.broadcast_to(lists[2 * i : 2 * i + 1, :], (8, slots))
        wide = jnp.concatenate([index] * SHARERS, 1)
        whole = jnp.where(lane >= base, pltpu.roll(wide, base, 1), whole) if i else wide
        base = base + lists[2 * i + 1, 0]
    for block in range(SHARERS):

        @pl.when(base > block * slots)
        def _():
            index = whole[:, block * slots : (block + 1) * slots]
            place = index & (LANES - 1)
            chunk = lax.shift_right_logical(index, LANE_BITS)

            def look(c, found):
                state = full[pl.ds(pl.multiple_of(c * 8, 8), 8), :]
                here = jnp.take_along_axis(state, place, axis=1, mode="promise_in_bounds")
                return jnp.where(chunk == c, here, found)

            found = lax.fori_loop(
                0, full.shape[0] // 8, look, jnp.zeros((8, slots), jnp.float32), unroll=16
            )
            for piece in range(0, slots, SPREAD):

                @pl.when(base > block * slots + piece)
                def _():
                    for row in range(piece, piece + SPREAD):
                        first = (block * slots + row) * 8
                        splat[first : first + 8, :] = jnp.broadcast_to(
                            found[:, row : row + 1], (8, LANES)
                        )


def group_bounds(lists):
    counts = [lists[2 * owner + 1, 0] for owner in range(SHARERS)]
    there, here = counts[0] + counts[1], counts[2] + counts[3]
    return (jnp.maximum(there, here) + 7) // 8, (there + here + 7) // 8


def add_lanes(begin, end, sums, flat):
    slots = flat.shape[1] // SHARERS
    for block in range(SHARERS):

        @pl.when((end * 8 > block * slots) & (begin * 8 < (block + 1) * slots))
        def _():
            part = pl.ds(block * slots, slots)
            for j in range(6):
                flat[pl.ds(j, 1), part] = jnp.sum(sums[j, part, :], axis=1)[None, :]


def cut(lists, owner, flat, slots):
    first = sum(lists[2 * before + 1, 0] for before in range(owner))
    return pltpu.roll(flat, flat.shape[1] - first, 1)[:, :slots] if owner else flat[:, :slots]


def add_forces(begin, end, splat, stars, chunks, stride, unroll, before, after, height=8):
    def group(g, _):
        place = pl.multiple_of(g * height, 8)
        rows = [
            jnp.concatenate(
                [splat[pl.ds((place + k) * 8 + i, 8, stride=8), :] for k in range(0, height, 8)], 0
            )
            for i in range(6)
        ]
        zero = jnp.zeros((height, LANES), jnp.float32)
        if before is None:
            total = (zero,) * 9
        else:
            total = tuple(before[i, pl.ds(place, height), :] for i in range(6)) + (zero,) * 3
        total = lax.fori_loop(
            0,
            chunks[1],
            lambda c, t: pair_terms(rows, stars, (chunks[0] + c) * stride, t),
            total,
            unroll=unroll,
        )
        for i in range(3):
            after[i, pl.ds(place, height), :] = total[i]
            after[3 + i, pl.ds(place, height), :] = total[3 + i] - 3.0 * total[6 + i]
        return _

    lax.fori_loop(begin, end, group, 0)


def near_kernel(lists, full, splat, sums):
    gather(lists, full, splat)
    _, groups = group_bounds(lists)
    size = full.shape[0] // (8 * SHARERS)
    place = lax.rem(lax.axis_index("group"), SHARERS)
    odd = lax.rem(place, 2)
    groups = (groups + 1) // 2
    first, less, more = place * size - odd * LEAN, size - LEAN, 2 * LEAN
    add_forces(0, groups, splat, full, (first, less), 8, less, None, sums, 16)
    add_forces(0, groups * odd, splat, full, (first + less, more), 8, more, sums, sums, 16)


def there_kernel(*refs):
    lists, splat, sums = refs[:3]
    parts, (blocks, flat, stars, held) = refs[3:-4], refs[-4:]
    begin = 0
    for part in parts:
        stars[pl.ds(begin, part.shape[0]), :] = part[...]
        begin += part.shape[0]
    shared, _ = group_bounds(lists)
    far = (0, stars.shape[0] // SENT)
    add_forces(0, shared, splat, stars, far, SENT, 48, sums, held)
    add_lanes(0, shared, held, flat)
    for owner in range(2):
        blocks[owner * 8 : owner * 8 + 8, :] = cut(lists, owner, flat[...], blocks.shape[1])


def here_kernel(lists, splat, sums, stars, flat, mine, other, held, rest):
    shared, groups = group_bounds(lists)
    far = (0, stars.shape[0] // SENT)
    add_forces(shared, groups, splat, stars, far, SENT, 48, sums, held)
    add_lanes(shared, groups, held, rest)
    done = lax.broadcasted_iota(jnp.int32, flat.shape, 1) < shared * 8
    whole = jnp.where(done, flat[...], rest[...])
    for owner, out in ((2, mine), (3, other)):
        out[...] = cut(lists, owner, whole, out.shape[1])


def on_device(
    star_pos, star_vel, star_acc, star_jerk, star_mass, star_dt, active_list, active_count
):
    n_blk = lax.axis_size("blk")
    n_group = lax.axis_size("group")
    shard = star_mass.shape[0]
    total_stars = shard * n_blk
    slots = active_list.shape[2]
    chunks = shard // LANES
    room = SHARERS * slots
    vmem = pl.BlockSpec(memory_space=pltpu.VMEM)
    smem = pl.BlockSpec(memory_space=pltpu.SMEM)
    params = pltpu.CompilerParams(vmem_limit_bytes=VMEM_LIMIT)
    splat_type = jax.ShapeDtypeStruct((room * 8, LANES), jnp.float32)
    sums_type = jax.ShapeDtypeStruct((6, room, LANES), jnp.float32)
    raw = (
        star_pos,
        star_vel,
        star_acc,
        star_jerk,
        star_mass.reshape(chunks, LANES),
        star_dt.reshape(chunks, LANES),
        active_list[0],
    )

    def swap(x, axis, bits):
        return lax.ppermute(x, axis, [(i, i ^ bits) for i in range(lax.axis_size(axis))])

    def trade(x, step):
        pairs = [
            (b * n_group + g, (b ^ step ^ (2 if g & 2 else 1)) * n_group + g)
            for b in range(n_blk)
            for g in range(n_group)
        ]
        return lax.ppermute(x, ("blk", "group"), pairs)

    part_type = jax.ShapeDtypeStruct((chunks * SENT // SHARERS, LANES), jnp.float32)
    full, part, half, packed = pl.pallas_call(
        functools.partial(predict_kernel, total_stars),
        out_shape=(
            jax.ShapeDtypeStruct((chunks * 8, LANES), jnp.float32),
            part_type,
            jax.ShapeDtypeStruct((chunks * SENT // 2, LANES), jnp.float32),
            jax.ShapeDtypeStruct((8, slots), jnp.int32),
        ),
        in_specs=[pl.BlockSpec(memory_space=pltpu.HBM)] * 7 + [smem],
        out_specs=(vmem,) * 4,
        scratch_shapes=[pltpu.VMEM(x.shape, x.dtype) for x in raw]
        + [pltpu.SemaphoreType.DMA((7,))],
        compiler_params=params,
        name="predict",
    )(*(pltpu.with_memory_space_constraint(x, pltpu.HBM) for x in raw), active_count)
    parts = []
    for step in range(0, n_blk, 4):
        parts.append(trade(half, step))
        parts += [swap(part, "blk", bits) for bits in (step + 3, step) if bits]
    core, *others = (swap(packed, "group", bits) for bits in range(1, SHARERS))
    lists = jnp.concatenate([x[:2] for x in (*others, packed, core)], 0)
    splat, sums = pl.pallas_call(
        near_kernel,
        out_shape=(splat_type, sums_type),
        in_specs=[vmem] * 2,
        out_specs=(vmem,) * 2,
        compiler_params=params,
        name="near_forces",
    )(lists, full)
    block_type = jax.ShapeDtypeStruct((8, slots), jnp.float32)
    pairs = slots * shard
    cost = pl.CostEstimate(flops=40 * pairs, bytes_accessed=pairs, transcendentals=pairs)
    flat_type = jax.ShapeDtypeStruct((8, SHARERS * slots), jnp.float32)
    stars_type = jax.ShapeDtypeStruct((sum(x.shape[0] for x in parts), LANES), jnp.float32)
    there, flat, stars = pl.pallas_call(
        there_kernel,
        out_shape=(
            jax.ShapeDtypeStruct((16, slots), jnp.float32),
            flat_type,
            stars_type,
        ),
        in_specs=[vmem] * (3 + len(parts)),
        out_specs=(vmem,) * 3,
        scratch_shapes=[pltpu.VMEM(sums_type.shape, jnp.float32)],
        compiler_params=params,
        cost_estimate=cost,
        name="there_forces",
    )(lists, splat, sums, *parts)
    returned = swap(there, "group", 2)
    mine, other = pl.pallas_call(
        here_kernel,
        out_shape=(block_type, block_type),
        in_specs=[vmem] * 5,
        out_specs=(vmem,) * 2,
        scratch_shapes=[
            pltpu.VMEM(sums_type.shape, jnp.float32),
            pltpu.VMEM(flat_type.shape, jnp.float32),
        ],
        compiler_params=params,
        cost_estimate=cost,
        name="here_forces",
    )(lists, splat, sums, stars, flat)
    total = mine + returned[:8] + swap(other + returned[8:], "group", 1)
    live = lax.broadcasted_iota(jnp.int32, (1, slots), 1) < packed[1:2]
    output = jnp.where(live, total[:6], 0.0)
    return output[None, None]


def solution(mesh):
    return jax.shard_map(
        on_device,
        mesh=mesh,
        in_specs=(
            P(None, "blk"),
            P(None, "blk"),
            P(None, "blk"),
            P(None, "blk"),
            P("blk"),
            P("blk"),
            P("blk", "group", None),
            P("blk", "group"),
        ),
        out_specs=P("blk", "group", None, None),
        check_vma=False,
    )
```
